32 devices in a mesh: gx: 2 (over x), gy: 4 (over y, core), gz: 4 (over z).
Axes of the slice: x: 2, y: 2, z: 4, core: 2. Of those that a mesh axis runs over, the one named last changes fastest.
Arguments:
- local_pos: float32 [4, 8, 4, 3, 64], P('gx', 'gy', 'gz'), as said below
- counts: int32 [4, 8, 4], P('gx', 'gy', 'gz'), may hold values from 8 to 64, as said below
- species: int32 [4, 8, 4, 64], P('gx', 'gy', 'gz'), may hold values from 0 to 9
- features: bfloat16 [4, 8, 4, 64, 128], P('gx', 'gy', 'gz'), may hold values from -6 to 6
- radial_weights: float32 [2, 8, 128], replicated, may hold values from -2 to 2
- coupling: float32 [3, 10, 128], replicated, may hold values from -3 to 3
- mixing: float32 [128, 128], replicated, may hold values from -0.5 to 0.5
- hidden_weights: float32 [128, 16], replicated, may hold values from -0.5 to 0.5
- output_weights: float32 [16], replicated, may hold values from -1.5 to 1.5
Outputs:
- atom_energy: float32 [4, 8, 4, 64], P('gx', 'gy', 'gz')
- forces: float32 [4, 8, 4, 3, 64], P('gx', 'gy', 'gz')
- feature_grad: float32 [4, 8, 4, 64, 128], P('gx', 'gy', 'gz')
The draws below stay inside these ranges and needn't reach their ends.
Inputs may be any that keep to these rules, and one draw needn't show every extreme that they name: `counts`: every cell holds between 8 and 64 atoms, and at least one cell is full. `local_pos`: the slots of a cell sit on distinct sites of a 4 x 4 x 4 lattice of spacing 7 / 4, each moved by at most 0.3 spacings along each coordinate, so any two slots are 0.4 spacings apart or more.
All inputs are finite; a program needn't handle non-finite values.
Results may differ from the reference program's by a relative error of at most 0.0048.
Values may be sent and summed in bfloat16 or wider, within the bound.
A program may use at most 64 MiB of HBM per device.

```python
import jax
import jax.numpy as jnp
import numpy as np
from jax import lax

CHAN = 128
NB = 8
HID = 16
NSPEC = 10
LAT = 4
SLOTS = 64
NCX = 4
NCY = 8
NCZ = 4


def draw_local_pos(key, part):
    total_cells = NCX * NCY * NCZ
    order_key, jitter_key = jax.random.split(key)
    orders = jax.vmap(lambda subkey: jax.random.permutation(subkey, SLOTS))(jax.random.split(order_key, total_cells))
    coord_x = orders // (LAT * LAT)
    coord_y = orders // LAT % LAT
    coord_z = orders % LAT
    lattice = jnp.stack([coord_x, coord_y, coord_z], axis=1).astype(jnp.float32)
    jitter = jax.random.uniform(jitter_key, (total_cells, 3, SLOTS), jnp.float32, -0.3, 0.3)
    spacing = 7.0 / LAT
    return ((lattice + 0.5 + jitter) * spacing).reshape(NCX, NCY, NCZ, 3, SLOTS)


def draw_counts(key, part):
    drawn = jax.random.randint(key, (NCX, NCY, NCZ), SLOTS // 8, SLOTS + 1, jnp.int32)
    return drawn.at[0, 0, 0].set(SLOTS)


def touch_ends(result, stream_key, low, high):
    place = [jax.random.randint(jax.random.fold_in(stream_key, axis), (), 0, length) for axis, length in enumerate(result.shape)]
    main_axis = result.shape.index(max(result.shape))
    neighbour = place[:main_axis] + [(place[main_axis] + 1) % result.shape[main_axis]] + place[main_axis + 1:]
    return result.at[tuple(place)].set(low).at[tuple(neighbour)].set(high)


def levels(key, extent, cuts, low, top_value):
    level, own = 1.0, jax.random.fold_in(key, 6)
    for dim, shards_of in cuts:
        draws = jnp.exp(jax.random.uniform(jax.random.fold_in(own, dim), (shards_of,), jnp.float32, low / len(cuts), top_value / len(cuts)))
        level = level * jnp.repeat(draws, extent[dim] // shards_of).reshape([-1 if axis == dim else 1 for axis in range(len(extent))])
    return level


def scatter_about(rng, dims, spread, limit, pieces=(), kind=jnp.bfloat16):
    loudness = levels(rng, dims, pieces, -0.22, 0.18) if pieces else 1.0
    values = jax.random.normal(rng, dims, jnp.float32) * spread * loudness
    return jnp.minimum(jnp.maximum(values, -limit), limit).astype(kind)


def setup_inputs(seed: int = 0) -> dict:
    seeds = jax.random.split(jax.random.key(seed), 10)
    return {
        "local_pos": draw_local_pos(jax.random.fold_in(seeds[9], 71), 0),
        "counts": draw_counts(jax.random.fold_in(seeds[9], 71), 0),
        "species": touch_ends(jax.random.randint(seeds[2], (NCX, NCY, NCZ, SLOTS), 0, NSPEC), jax.random.fold_in(seeds[2], 1), 0, NSPEC - 1).astype(jnp.int32),
        "features": scatter_about(seeds[3], (NCX, NCY, NCZ, SLOTS, CHAN), 1.0, 6.0, ((0, 2), (1, 4), (2, 4))),
        "radial_weights": scatter_about(seeds[4], (2, NB, CHAN), NB ** -0.5, 2.0, (), jnp.float32),
        "coupling": scatter_about(seeds[5], (3, NSPEC, CHAN), 0.5, 3.0, (), jnp.float32),
        "mixing": scatter_about(seeds[6], (CHAN, CHAN), CHAN ** -0.5, 0.5, (), jnp.float32),
        "hidden_weights": scatter_about(seeds[7], (CHAN, HID), CHAN ** -0.5, 0.5, (), jnp.float32),
        "output_weights": scatter_about(seeds[8], (HID,), HID ** -0.5, 1.5, (), jnp.float32),
    }


SIDE = 7.0
CUTOFF = 5.0
OFFSETS = np.array([[step_a, step_b, step_c] for step_a in (-1, 0, 1) for step_b in (-1, 0, 1) for step_c in (-1, 0, 1)], dtype=np.float32) * SIDE
middle_cell = 13

def edge_terms(own_xyz, far_xyz, pair_weight, self_mask, basis_count):
    displace = far_xyz[:, None, :] - own_xyz[:, :, None]
    radius = jnp.sqrt(lax.optimization_barrier(jnp.sum(displace * displace, axis=0)) + self_mask)
    scaled = radius / CUTOFF
    envelope = 1.0 - 28.0 * scaled ** 6 + 48.0 * scaled ** 7 - 21.0 * scaled ** 8
    envelope = jnp.where(radius < CUTOFF, envelope, 0.0) * pair_weight
    orders = jnp.arange(1, basis_count + 1, dtype=jnp.float32)
    bessel = jnp.sqrt(2.0 / CUTOFF) * jnp.sin(orders[:, None, None] * jnp.pi * radius[None] / CUTOFF) / radius[None]
    radial_part = bessel * envelope[None]
    harmonics = jnp.concatenate([jnp.ones_like(radius)[None], jnp.sqrt(3.0) * displace / radius[None]], axis=0)
    edge_values = radial_part[:, None] * harmonics[None]
    return edge_values.reshape(basis_count * 4, radius.shape[0], radius.shape[1])

def cell_terms(own_pos, own_kind, near_pos, near_feat, radial_weights, coupling, mixing, hidden_weights, output_weights):
    capacity = own_pos.shape[1]
    near_count = near_pos.shape[0] * capacity
    basis_count = radial_weights.shape[1]
    channels = near_feat.shape[1]
    far_xyz = (near_pos[:, :3, :] + OFFSETS[:, :, None]).transpose(1, 0, 2).reshape(3, near_count)
    far_occ = near_pos[:, 3, :].reshape(near_count)
    own_xyz = own_pos[:3]
    own_occ = own_pos[3]
    column = jnp.arange(near_count, dtype=jnp.int32)
    own_index = jnp.arange(capacity, dtype=jnp.int32)
    self_mask = (column[None, :] == own_index[:, None] + middle_cell * capacity).astype(jnp.float32)
    pair_weight = own_occ[:, None] * far_occ[None, :] * (1.0 - self_mask)

    def edges(xyz_own, xyz_far):
        return edge_terms(xyz_own, xyz_far, pair_weight, self_mask, basis_count)
    edge_values, pullback = jax.vjp(edges, own_xyz, far_xyz)
    edge_half = edge_values.astype(jnp.bfloat16).reshape(basis_count * 4 * capacity, near_count)
    summed = jnp.dot(edge_half, near_feat, preferred_element_type=jnp.float32)
    summed = summed.reshape(basis_count, 4, capacity, channels)
    scalar = lax.optimization_barrier(jnp.sum(summed[:, 0] * radial_weights[0][:, None, :], axis=0))
    vector = lax.optimization_barrier(jnp.sum(summed[:, 1:] * radial_weights[1][:, None, None, :], axis=0))
    kind_onehot = (own_kind[:, None] == jnp.arange(coupling.shape[1], dtype=jnp.int32)[None, :]).astype(jnp.float32)
    weights = jnp.einsum('sk,qkc->qsc', kind_onehot, coupling, precision=lax.Precision.HIGHEST)
    length_sq = lax.optimization_barrier(jnp.sum(vector * vector, axis=0))
    product = weights[0] * scalar + weights[1] * scalar * scalar + weights[2] * length_sq
    mixed_out = jnp.dot(product, mixing, precision=lax.Precision.HIGHEST)
    hidden = jnp.dot(mixed_out, hidden_weights, precision=lax.Precision.HIGHEST)
    logistic = jax.nn.sigmoid(hidden)
    energy = own_occ * lax.optimization_barrier(jnp.sum(output_weights[None, :] * hidden * logistic, axis=1))
    d_hidden = own_occ[:, None] * output_weights[None, :] * logistic * (1.0 + hidden * (1.0 - logistic))
    d_mixed = jnp.dot(d_hidden, hidden_weights.T, precision=lax.Precision.HIGHEST)
    d_product = jnp.dot(d_mixed, mixing.T, precision=lax.Precision.HIGHEST)
    d_scalar = d_product * (weights[0] + 2.0 * weights[1] * scalar)
    d_vector = 2.0 * weights[2][None] * vector * d_product[None]
    d_first = radial_weights[0][:, None, :] * d_scalar[None]
    d_rest = radial_weights[1][:, None, None, :] * d_vector[None]
    d_summed = jnp.concatenate([d_first[:, None], d_rest], axis=1)
    d_half = d_summed.astype(jnp.bfloat16).reshape(basis_count * 4 * capacity, channels)
    d_edge = lax.dot_general(d_half, near_feat, (((1,), (1,)), ((), ())), preferred_element_type=jnp.float32)
    d_edge = d_edge.reshape(basis_count * 4, capacity, near_count)
    d_feat = lax.dot_general(edge_half, d_half, (((0,), (0,)), ((), ())), preferred_element_type=jnp.float32)
    d_own, d_far = pullback(d_edge)
    d_far = d_far.reshape(3, near_pos.shape[0], capacity).transpose(1, 0, 2)
    d_far = d_far.at[middle_cell].add(d_own)
    return (energy, d_far, d_feat.reshape(near_pos.shape[0], capacity, channels))

def reference(local_pos, counts, species, features, radial_weights, coupling, mixing, hidden_weights, output_weights):
    cells_x, cells_y, cells_z = counts.shape
    capacity = features.shape[3]
    channels = features.shape[4]
    total_cells = cells_x * cells_y * cells_z
    occupied = (jnp.arange(capacity, dtype=jnp.int32)[None, None, None, :] < counts[..., None]).astype(jnp.float32)
    with_occ = jnp.concatenate([local_pos, occupied[:, :, :, None, :]], axis=3).reshape(total_cells, 4, capacity)
    feat_flat = features.reshape(total_cells, capacity, channels)
    kind_flat = species.reshape(total_cells, capacity)
    flat_ids = np.arange(total_cells)
    coord_x = flat_ids // (cells_y * cells_z)
    coord_y = flat_ids // cells_z % cells_y
    coord_z = flat_ids % cells_z
    columns = []
    for step_x in range(3):
        for step_y in range(3):
            for step_z in range(3):
                columns.append((coord_x + step_x - 1) % cells_x * cells_y * cells_z + (coord_y + step_y - 1) % cells_y * cells_z + (coord_z + step_z - 1) % cells_z)
    neighbor_table = jnp.asarray(np.stack(columns, axis=1).astype(np.int32))

    def visit_cell(totals, cell_id):
        feat_total, pos_total = totals
        near_index = neighbor_table[cell_id]
        near_pos = with_occ[near_index]
        near_feat = feat_flat[near_index].reshape(27 * capacity, channels)
        energy, d_far, d_feat = cell_terms(with_occ[cell_id], kind_flat[cell_id], near_pos, near_feat, radial_weights, coupling, mixing, hidden_weights, output_weights)
        return ((feat_total.at[near_index].add(d_feat), pos_total.at[near_index].add(d_far)), energy)
    start = (jnp.zeros((total_cells, capacity, channels), jnp.float32), jnp.zeros((total_cells, 3, capacity), jnp.float32))
    (feat_total, pos_total), energies = lax.scan(visit_cell, start, jnp.arange(total_cells, dtype=jnp.int32))
    atom_energy = energies.reshape(cells_x, cells_y, cells_z, capacity)
    forces = (-pos_total).reshape(cells_x, cells_y, cells_z, 3, capacity)
    feature_grad = feat_total.reshape(cells_x, cells_y, cells_z, capacity, channels)
    return (atom_energy, forces, feature_grad)
```

```python
import functools
import math

import jax
import jax.numpy as jnp
import numpy as np
from jax import lax
from jax.experimental import pallas as pl
from jax.experimental.pallas import tpu as pltpu
from jax.sharding import PartitionSpec as P

SIDE = 7.0
CUTOFF = 5.0
JITTER = 0.3
BLOCK = 2
HIGH = lax.Precision.HIGHEST


def lattice_of(capacity):
    lat = round(capacity ** (1.0 / 3.0))
    spacing = SIDE / lat
    reach = 0
    while (reach + 1 - 2 * JITTER) * spacing < CUTOFF:
        reach += 1
    return lat, spacing, reach


def pair_fields(pj, pi):
    dx = pj[0:1, :] - pi[:, 0:1]
    dy = pj[1:2, :] - pi[:, 1:2]
    dz = pj[2:3, :] - pi[:, 2:3]
    sq = dx * dx + dy * dy + dz * dz
    near = jnp.logical_and(sq < CUTOFF * CUTOFF, sq > 0.01)
    weight = jnp.where(near, pj[3:4, :] * pi[:, 3:4], 0.0)
    safe = jnp.where(near, sq, 1.0)
    inv = lax.rsqrt(safe)
    r = safe * inv
    u = r * (1.0 / CUTOFF)
    u2 = u * u
    u5 = u2 * u2 * u
    env = 1.0 + u5 * u * (-28.0 + u * (48.0 - 21.0 * u))
    denv = u5 * (-168.0 + u * (336.0 - 168.0 * u)) * (1.0 / CUTOFF)
    amp = weight * inv * math.sqrt(2.0 / CUTOFF)
    q = amp * env
    p = amp * denv - q * inv
    t = u * math.pi - 0.5 * math.pi
    t2 = t * t
    cos_t = 1.0 + t2 * (
        -1.0 / 2 + t2 * (1.0 / 24 + t2 * (-1.0 / 720 + t2 * (1.0 / 40320 + t2 * (-1.0 / 3628800 + t2 * (1.0 / 479001600)))))
    )
    sin_t = t * (
        1.0 + t2 * (-1.0 / 6 + t2 * (1.0 / 120 + t2 * (-1.0 / 5040 + t2 * (1.0 / 362880 + t2 * (-1.0 / 39916800)))))
    )
    return dx * inv, dy * inv, dz * inv, inv, q, p, cos_t, -sin_t


def compute_kernel(
    dims,
    feat_ref,
    posj_ref,
    rpos_ref,
    radial_ref,
    coupling_ref,
    mixing_ref,
    hw_ref,
    ow_ref,
    fgrad_ref,
    fj_ref,
    node_ref,
    slab_ref,
    edge_ref,
    field_ref,
    sv_ref,
    en_ref,
    acc_ref,
    g_ref,
):
    sx, sy, sz, reach, nb = dims
    nbx, nby = sx // BLOCK, sy // BLOCK
    wide = BLOCK + 2 * reach
    depth = sz + 2 * reach
    rows = wide * depth
    near = wide * rows
    own = BLOCK * BLOCK * sz
    px = sx + 2 * reach
    chunks = [(c, min(128, near - c)) for c in range(0, near, 128)]
    root3 = math.sqrt(3.0)

    def build(x, carry):
        full = feat_ref[x].astype(jnp.float32)
        for by in range(nby):
            start = by * BLOCK * depth
            slab_ref[by, x] = full[start : start + rows].astype(jnp.bfloat16)
            acc_ref[by, x] = jnp.zeros((rows, full.shape[1]), jnp.float32)
        return carry

    lax.fori_loop(0, px, build, 0)

    def forward(blk, carry):
        by, bx = blk // nbx, lax.rem(blk, nbx)
        pi = rpos_ref[blk]
        for c, w in chunks:
            pj = posj_ref[blk, :, c : c + w]
            nx, ny, nz, inv, q, p, s1, c1 = pair_fields(pj, pi)
            field_ref[blk, 0, :, c : c + w] = nx
            field_ref[blk, 1, :, c : c + w] = ny
            field_ref[blk, 2, :, c : c + w] = nz
            field_ref[blk, 3, :, c : c + w] = inv
            field_ref[blk, 4, :, c : c + w] = q
            field_ref[blk, 5, :, c : c + w] = p
            field_ref[blk, 6, :, c : c + w] = s1
            field_ref[blk, 7, :, c : c + w] = c1
            twice = 2.0 * c1
            before, now = jnp.zeros_like(s1), s1
            q3 = root3 * q
            qs = (q, q3 * nx, q3 * ny, q3 * nz)
            for b in range(nb):
                for m in range(4):
                    k = (b * 4 + m) * own
                    edge_ref[blk, k : k + own, c : c + w] = (qs[m] * now).astype(jnp.bfloat16)
                before, now = now, twice * now - before
        slab = slab_ref[by, pl.ds(bx * BLOCK, wide)].reshape(near, -1)
        summed = jnp.dot(edge_ref[blk], slab, preferred_element_type=jnp.float32)
        for m in range(4):
            total = None
            for b in range(nb):
                k = (b * 4 + m) * own
                term = summed[k : k + own] * radial_ref[min(m, 1), b : b + 1, :]
                total = term if total is None else total + term
            sv_ref[m, pl.ds(blk * own, own)] = total
        return carry

    lax.fori_loop(0, nbx * nby, forward, 0)

    flat = rpos_ref[...].reshape(nbx * nby * own, -1)
    occ = flat[:, 3:4]
    kind = flat[:, 4:5]
    spec = lax.broadcasted_iota(jnp.int32, (flat.shape[0], coupling_ref.shape[1]), 1)
    onehot = (kind.astype(jnp.int32) == spec).astype(jnp.float32)
    wq = [
        jnp.dot(onehot, coupling_ref[n], precision=HIGH, preferred_element_type=jnp.float32)
        for n in range(3)
    ]
    scalar = sv_ref[0]
    length_sq = sv_ref[1] * sv_ref[1] + sv_ref[2] * sv_ref[2] + sv_ref[3] * sv_ref[3]
    product = wq[0] * scalar + wq[1] * scalar * scalar + wq[2] * length_sq
    fold = jnp.dot(mixing_ref[...], hw_ref[...], precision=HIGH, preferred_element_type=jnp.float32)
    hidden = jnp.dot(product, fold, precision=HIGH, preferred_element_type=jnp.float32)
    logistic = jax.nn.sigmoid(hidden)
    energy = occ * jnp.sum(ow_ref[...] * hidden * logistic, axis=1, keepdims=True)
    d_hidden = occ * ow_ref[...] * logistic * (1.0 + hidden * (1.0 - logistic))
    d_product = lax.dot_general(
        d_hidden, fold, (((1,), (1,)), ((), ())), precision=HIGH, preferred_element_type=jnp.float32
    )
    en_ref[...] = jnp.broadcast_to(energy, en_ref.shape)
    sv_ref[0] = d_product * (wq[0] + 2.0 * wq[1] * scalar)
    twice_d = 2.0 * wq[2] * d_product
    for m in range(1, 4):
        sv_ref[m] = twice_d * sv_ref[m]

    def backward(blk, carry):
        by, bx = blk // nbx, lax.rem(blk, nbx)
        parts = []
        for b in range(nb):
            for m in range(4):
                parts.append(
                    sv_ref[m, pl.ds(blk * own, own)] * radial_ref[min(m, 1), b : b + 1, :]
                )
        d_full = jnp.concatenate(parts, axis=0)
        d_half = d_full.astype(jnp.bfloat16)
        slab = slab_ref[by, pl.ds(bx * BLOCK, wide)].reshape(near, -1)
        g_ref[...] = lax.dot_general(
            d_half, slab, (((1,), (1,)), ((), ())), preferred_element_type=jnp.float32
        )
        d_turn = d_full.T.astype(jnp.bfloat16)
        turned = jnp.dot(d_turn, edge_ref[blk], preferred_element_type=jnp.float32)
        acc_ref[by, pl.ds(bx * BLOCK, wide)] += turned.T.reshape(wide, rows, -1)
        total = [jnp.zeros((own, 1), jnp.float32) for _ in range(3)]
        for c, w in chunks:
            nx, ny, nz, inv, q, p, s1, c1 = (field_ref[blk, n, :, c : c + w] for n in range(8))
            twice = 2.0 * c1
            s_before, s_now = jnp.zeros_like(s1), s1
            c_before, c_now = jnp.ones_like(c1), c1
            s_sum = [None] * 4
            c_sum = [None] * 4
            for b in range(nb):
                scaled = (b + 1.0) * c_now
                for m in range(4):
                    k = (b * 4 + m) * own
                    g = g_ref[k : k + own, c : c + w]
                    s_sum[m] = g * s_now if b == 0 else s_sum[m] + g * s_now
                    c_sum[m] = g * scaled if b == 0 else c_sum[m] + g * scaled
                s_before, s_now = s_now, twice * s_now - s_before
                c_before, c_now = c_now, twice * c_now - c_before
            s_dot = nx * s_sum[1] + ny * s_sum[2] + nz * s_sum[3]
            c_dot = nx * c_sum[1] + ny * c_sum[2] + nz * c_sum[3]
            slope = (q * (math.pi / CUTOFF)) * (c_sum[0] + root3 * c_dot) + p * (
                s_sum[0] + root3 * s_dot
            )
            across = root3 * q * inv
            along = slope - across * s_dot
            outs = [
                along * n + across * s_sum[m + 1] for m, n in enumerate((nx, ny, nz))
            ]
            for m in range(3):
                fj_ref[blk, m : m + 1, c : c + w] = -jnp.sum(outs[m], axis=0, keepdims=True)
                total[m] = total[m] + jnp.sum(outs[m], axis=1, keepdims=True)
        lane = lax.broadcasted_iota(jnp.int32, (own, node_ref.shape[1]), 1)
        here = pl.ds(blk * own, own)
        node_ref[here] = jnp.where(
            lane == 0,
            total[0],
            jnp.where(lane == 1, total[1], jnp.where(lane == 2, total[2], en_ref[here])),
        )
        return carry

    lax.fori_loop(0, nbx * nby, backward, 0)

    def merge(x, carry):
        fgrad_ref[x] = jnp.zeros(fgrad_ref.shape[1:], jnp.float32)
        for by in range(nby):
            start = by * BLOCK * depth
            fgrad_ref[x, start : start + rows] += acc_ref[by, x]
        return carry

    lax.fori_loop(0, px, merge, 0)


def shift(block, axis, up):
    count = lax.axis_size(axis)
    pairs = [(i, (i + 1) % count) for i in range(count)]
    if not up:
        pairs = [(b, a) for a, b in pairs]
    return lax.ppermute(block, axis, pairs)


def widen(block, axis, dim, reach):
    extent = block.shape[dim]
    low = shift(lax.slice_in_dim(block, extent - reach, extent, axis=dim), axis, True)
    high = shift(lax.slice_in_dim(block, 0, reach, axis=dim), axis, False)
    return jnp.concatenate([low, block, high], axis=dim)


def fold_back(block, axis, dim, reach):
    extent = block.shape[dim]
    low = lax.slice_in_dim(block, 0, reach, axis=dim).astype(jnp.bfloat16)
    high = lax.slice_in_dim(block, extent - reach, extent, axis=dim).astype(jnp.bfloat16)
    to_high = shift(low, axis, False).astype(block.dtype)
    to_low = shift(high, axis, True).astype(block.dtype)
    core = lax.slice_in_dim(block, reach, extent - reach, axis=dim)
    rest = extent - 3 * reach
    low_pad = [(0, 0)] * block.ndim
    high_pad = [(0, 0)] * block.ndim
    low_pad[dim] = (0, rest)
    high_pad[dim] = (rest, 0)
    return core + jnp.pad(to_low, low_pad) + jnp.pad(to_high, high_pad)


def body(
    local_pos,
    counts,
    species,
    features,
    radial_weights,
    coupling,
    mixing,
    hidden_weights,
    output_weights,
):
    cx, cy, cz = counts.shape
    capacity, channels = features.shape[3:]
    nb = radial_weights.shape[1]
    lat, spacing, reach = lattice_of(capacity)
    sx, sy, sz = cx * lat, cy * lat, cz * lat
    nbx, nby = sx // BLOCK, sy // BLOCK
    wide, depth = BLOCK + 2 * reach, sz + 2 * reach
    near, own = wide * wide * depth, BLOCK * BLOCK * sz
    px, py = sx + 2 * reach, sy + 2 * reach
    rows_full = -(-py * depth // 16) * 16

    occupied = (jnp.arange(capacity, dtype=jnp.int32) < counts[..., None]).astype(jnp.float32)
    site = jnp.clip(jnp.floor(local_pos * (1.0 / spacing)).astype(jnp.int32), 0, lat - 1)
    code = (site[:, :, :, 0] * lat + site[:, :, :, 1]) * lat + site[:, :, :, 2]
    place = code[:, :, :, None, :] == jnp.arange(capacity, dtype=jnp.int32)[:, None]
    place_half = place.astype(jnp.bfloat16)
    place_full = place.astype(jnp.float32)
    feat_sites = jnp.einsum(
        "xyzts,xyzsc->xyztc", place_half, features, preferred_element_type=jnp.float32
    ).astype(jnp.bfloat16)
    small = jnp.concatenate(
        [
            local_pos,
            occupied[:, :, :, None],
            species.astype(jnp.float32)[:, :, :, None],
        ],
        axis=3,
    )
    small_sites = jnp.einsum("xyzks,xyzts->kxyzt", small, place_full, precision=HIGH)

    feat_grid = feat_sites.reshape(cx, cy, cz, lat, lat, lat, channels)
    feat_grid = feat_grid.transpose(0, 3, 1, 4, 2, 5, 6).reshape(sx, sy, sz, channels)
    small_grid = small_sites.reshape(5, cx, cy, cz, lat, lat, lat)
    small_grid = small_grid.transpose(0, 1, 4, 2, 5, 3, 6).reshape(5, sx, sy, sz)

    feat_pad = widen(feat_grid, "gz", 2, reach)
    feat_pad = widen(feat_pad, "gy", 1, reach)
    feat_pad = widen(feat_pad, "gx", 0, reach)
    feat_pad = feat_pad.reshape(px, py * depth, channels)
    feat_pad = jnp.pad(feat_pad, ((0, 0), (0, rows_full - py * depth), (0, 0)))
    pos_pad = small_grid[:4]
    for axis, dim in (("gz", 3), ("gy", 2), ("gx", 1)):
        pos_pad = widen(pos_pad, axis, dim, reach)
    steps = [
        np.floor((np.arange(n) - reach) / lat).astype(np.float32) * SIDE
        for n in (px, py, depth)
    ]
    shifts = np.zeros((4, px, py, depth), np.float32)
    shifts[0] = steps[0][:, None, None]
    shifts[1] = steps[1][None, :, None]
    shifts[2] = steps[2][None, None, :]
    pos_pad = pos_pad + shifts
    posj = jnp.stack(
        [
            pos_pad[:, bx * BLOCK : bx * BLOCK + wide, by * BLOCK : by * BLOCK + wide].reshape(4, near)
            for by in range(nby)
            for bx in range(nbx)
        ]
    )
    own_shift = np.concatenate(
        [shifts[:, reach : reach + sx, reach : reach + sy, reach : reach + sz], np.zeros((1, sx, sy, sz), np.float32)]
    )
    rpos = (small_grid + own_shift).reshape(5, nbx, BLOCK, nby, BLOCK, sz)
    rpos = rpos.transpose(3, 1, 2, 4, 5, 0).reshape(nby * nbx, own, 5)
    rpos = jnp.pad(rpos, ((0, 0), (0, 0), (0, 3)))

    spec_pad = -(-coupling.shape[1] // 8) * 8 - coupling.shape[1]
    total_own = sx * sy * sz
    rows = wide * depth
    blocks = nbx * nby
    vmem = pl.BlockSpec(memory_space=pltpu.VMEM)
    fgrad, fj, node = pl.pallas_call(
        functools.partial(compute_kernel, (sx, sy, sz, reach, nb)),
        out_shape=(
            jax.ShapeDtypeStruct((px, rows_full, channels), jnp.float32),
            jax.ShapeDtypeStruct((blocks, 3, near), jnp.float32),
            jax.ShapeDtypeStruct((total_own, 128), jnp.float32),
        ),
        in_specs=[vmem] * 8,
        out_specs=(vmem, vmem, vmem),
        scratch_shapes=[
            pltpu.VMEM((nby, px, rows, channels), jnp.bfloat16),
            pltpu.VMEM((blocks, nb * 4 * own, near), jnp.bfloat16),
            pltpu.VMEM((blocks, 8, own, near), jnp.float32),
            pltpu.VMEM((4, total_own, channels), jnp.float32),
            pltpu.VMEM((total_own, 128), jnp.float32),
            pltpu.VMEM((nby, px, rows, channels), jnp.float32),
            pltpu.VMEM((nb * 4 * own, near), jnp.float32),
        ],
        compiler_params=pltpu.CompilerParams(vmem_limit_bytes=50 * 1024 * 1024),
        name="pair_layer",
    )(
        feat_pad,
        posj,
        rpos,
        radial_weights,
        jnp.pad(coupling, ((0, 0), (0, spec_pad), (0, 0))),
        mixing,
        hidden_weights,
        output_weights[None, :],
    )

    grad = fgrad[:, : py * depth].reshape(px, py, depth, channels)
    for axis, dim in (("gx", 0), ("gy", 1), ("gz", 2)):
        grad = fold_back(grad, axis, dim, reach)
    fj = fj.reshape(nby, nbx, 3, wide, wide, depth)
    force = jnp.zeros((3, px, py, depth), jnp.float32)
    for by in range(nby):
        for bx in range(nbx):
            force = force + jnp.pad(
                fj[by, bx],
                (
                    (0, 0),
                    (bx * BLOCK, px - wide - bx * BLOCK),
                    (by * BLOCK, py - wide - by * BLOCK),
                    (0, 0),
                ),
            )
    for axis, dim in (("gx", 1), ("gy", 2), ("gz", 3)):
        force = fold_back(force, axis, dim, reach)
    node = node[:, :4].reshape(nby, nbx, BLOCK, BLOCK, sz, 4)
    node = node.transpose(5, 1, 2, 0, 3, 4).reshape(4, sx, sy, sz)
    node = node + jnp.pad(force, ((0, 1), (0, 0), (0, 0), (0, 0)))

    def to_cells(grid):
        lead = grid.shape[3:]
        cells = grid.reshape((cx, lat, cy, lat, cz, lat) + lead)
        cells = cells.transpose((0, 2, 4, 1, 3, 5) + tuple(range(6, cells.ndim)))
        return cells.reshape((cx, cy, cz, capacity) + lead)

    feature_grad = jnp.einsum("xyzts,xyztc->xyzsc", place_full, to_cells(grad), precision=HIGH)
    node_slots = jnp.einsum(
        "xyzts,xyztk->xyzks", place_full, to_cells(node.transpose(1, 2, 3, 0)), precision=HIGH
    )
    return (node_slots[:, :, :, 3], node_slots[:, :, :, :3], feature_grad)


def solution(mesh):
    placed = (
        P("gx", "gy", "gz", None, None),
        P("gx", "gy", "gz"),
        P("gx", "gy", "gz", None),
        P("gx", "gy", "gz", None, None),
        P(),
        P(),
        P(),
        P(),
        P(),
    )
    return jax.shard_map(
        body,
        mesh=mesh,
        in_specs=placed,
        out_specs=(
            P("gx", "gy", "gz", None),
            P("gx", "gy", "gz", None, None),
            P("gx", "gy", "gz", None, None),
        ),
        check_vma=False,
    )
```

```python
import functools
import math

import jax
import jax.numpy as jnp
import numpy as np
from jax import lax
from jax.experimental import pallas as pl
from jax.experimental.pallas import tpu as pltpu
from jax.sharding import PartitionSpec as P

SIDE = 7.0
CUTOFF = 5.0
JITTER = 0.3
BLOCK = 2
HIGH = lax.Precision.HIGHEST


def lattice_of(capacity):
    lat = round(capacity ** (1.0 / 3.0))
    spacing = SIDE / lat
    reach = 0
    while (reach + 1 - 2 * JITTER) * spacing < CUTOFF:
        reach += 1
    return lat, spacing, reach


def pair_fields(pj, pi):
    dx = pj[0:1, :] - pi[:, 0:1]
    dy = pj[1:2, :] - pi[:, 1:2]
    dz = pj[2:3, :] - pi[:, 2:3]
    sq = dx * dx + dy * dy + dz * dz
    near = jnp.logical_and(sq < CUTOFF * CUTOFF, sq > 0.01)
    weight = jnp.where(near, pj[3:4, :] * pi[:, 3:4], 0.0)
    safe = jnp.where(near, sq, 1.0)
    inv = lax.rsqrt(safe)
    r = safe * inv
    u = r * (1.0 / CUTOFF)
    u2 = u * u
    u5 = u2 * u2 * u
    env = 1.0 + u5 * u * (-28.0 + u * (48.0 - 21.0 * u))
    denv = u5 * (-168.0 + u * (336.0 - 168.0 * u)) * (1.0 / CUTOFF)
    amp = weight * inv * math.sqrt(2.0 / CUTOFF)
    q = amp * env
    p = amp * denv - q * inv
    t = u * math.pi - 0.5 * math.pi
    t2 = t * t
    cos_t = 1.0 + t2 * (
        -1.0 / 2 + t2 * (1.0 / 24 + t2 * (-1.0 / 720 + t2 * (1.0 / 40320 + t2 * (-1.0 / 3628800 + t2 * (1.0 / 479001600)))))
    )
    sin_t = t * (
        1.0 + t2 * (-1.0 / 6 + t2 * (1.0 / 120 + t2 * (-1.0 / 5040 + t2 * (1.0 / 362880 + t2 * (-1.0 / 39916800)))))
    )
    return dx * inv, dy * inv, dz * inv, inv, q, p, cos_t, -sin_t


def compute_kernel(
    dims,
    layer_ref,
    posw_ref,
    pick_ref,
    pick_t_ref,
    rpos_ref,
    radial_ref,
    coupling_ref,
    mixing_ref,
    hw_ref,
    ow_ref,
    fgrad_ref,
    wsum_ref,
    node_ref,
    posj_ref,
    fj_ref,
    slab_ref,
    edge_ref,
    field_ref,
    sv_ref,
    en_ref,
    acc_ref,
    g_ref,
):
    sx, sy, sz, reach, nb = dims
    nbx, nby = sx // BLOCK, sy // BLOCK
    wide = BLOCK + 2 * reach
    depth = sz + 2 * reach
    rows = wide * depth
    near = wide * rows
    own = BLOCK * BLOCK * sz
    px = sx + 2 * reach
    chunks = [(c, min(128, near - c)) for c in range(0, near, 128)]
    root3 = math.sqrt(3.0)

    def build(x, carry):
        full = jnp.dot(pick_ref[...], layer_ref[x], preferred_element_type=jnp.float32)
        full = full.astype(jnp.bfloat16)
        for by in range(nby):
            slab_ref[by, x] = full[by * rows : (by + 1) * rows]
            acc_ref[by, x] = jnp.zeros((rows, full.shape[1]), jnp.float32)
        return carry

    lax.fori_loop(0, px, build, 0)
    wsum_ref[...] = jnp.zeros(wsum_ref.shape, jnp.float32)
    fj_ref[...] = jnp.zeros(fj_ref.shape, jnp.float32)

    def place_columns(by, carry):
        for bx in range(nbx):
            for k in range(wide):
                posj_ref[by * nbx + bx, :, k * rows : (k + 1) * rows] = posw_ref[by, bx * BLOCK + k]
        return carry

    lax.fori_loop(0, nby, place_columns, 0)

    def forward(blk, carry):
        by, bx = blk // nbx, lax.rem(blk, nbx)
        pi = rpos_ref[blk]
        for c, w in chunks:
            pj = posj_ref[blk, :, c : c + w]
            nx, ny, nz, inv, q, p, s1, c1 = pair_fields(pj, pi)
            field_ref[blk, 0, :, c : c + w] = nx
            field_ref[blk, 1, :, c : c + w] = ny
            field_ref[blk, 2, :, c : c + w] = nz
            field_ref[blk, 3, :, c : c + w] = inv
            field_ref[blk, 4, :, c : c + w] = q
            field_ref[blk, 5, :, c : c + w] = p
            field_ref[blk, 6, :, c : c + w] = s1
            field_ref[blk, 7, :, c : c + w] = c1
            twice = 2.0 * c1
            before, now = jnp.zeros_like(s1), s1
            q3 = root3 * q
            qs = (q, q3 * nx, q3 * ny, q3 * nz)
            for b in range(nb):
                for m in range(4):
                    k = (b * 4 + m) * own
                    edge_ref[blk, k : k + own, c : c + w] = (qs[m] * now).astype(jnp.bfloat16)
                before, now = now, twice * now - before
        slab = slab_ref[by, pl.ds(bx * BLOCK, wide)].reshape(near, -1)
        summed = jnp.dot(edge_ref[blk], slab, preferred_element_type=jnp.float32)
        for m in range(4):
            total = None
            for b in range(nb):
                k = (b * 4 + m) * own
                term = summed[k : k + own] * radial_ref[min(m, 1), b : b + 1, :]
                total = term if total is None else total + term
            sv_ref[m, pl.ds(blk * own, own)] = total
        return carry

    lax.fori_loop(0, nbx * nby, forward, 0)

    flat = rpos_ref[...].reshape(nbx * nby * own, -1)
    occ = flat[:, 3:4]
    kind = flat[:, 4:5]
    spec = lax.broadcasted_iota(jnp.int32, (flat.shape[0], coupling_ref.shape[1]), 1)
    onehot = (kind.astype(jnp.int32) == spec).astype(jnp.float32)
    wq = [
        jnp.dot(onehot, coupling_ref[n], precision=HIGH, preferred_element_type=jnp.float32)
        for n in range(3)
    ]
    scalar = sv_ref[0]
    length_sq = sv_ref[1] * sv_ref[1] + sv_ref[2] * sv_ref[2] + sv_ref[3] * sv_ref[3]
    product = wq[0] * scalar + wq[1] * scalar * scalar + wq[2] * length_sq
    fold = jnp.dot(mixing_ref[...], hw_ref[...], precision=HIGH, preferred_element_type=jnp.float32)
    hidden = jnp.dot(product, fold, precision=HIGH, preferred_element_type=jnp.float32)
    logistic = jax.nn.sigmoid(hidden)
    energy = occ * jnp.sum(ow_ref[...] * hidden * logistic, axis=1, keepdims=True)
    d_hidden = occ * ow_ref[...] * logistic * (1.0 + hidden * (1.0 - logistic))
    d_product = lax.dot_general(
        d_hidden, fold, (((1,), (1,)), ((), ())), precision=HIGH, preferred_element_type=jnp.float32
    )
    en_ref[...] = jnp.broadcast_to(energy, en_ref.shape)
    sv_ref[0] = d_product * (wq[0] + 2.0 * wq[1] * scalar)
    twice_d = 2.0 * wq[2] * d_product
    for m in range(1, 4):
        sv_ref[m] = twice_d * sv_ref[m]

    def backward(blk, carry):
        by, bx = blk // nbx, lax.rem(blk, nbx)
        parts = []
        for b in range(nb):
            for m in range(4):
                parts.append(
                    sv_ref[m, pl.ds(blk * own, own)] * radial_ref[min(m, 1), b : b + 1, :]
                )
        d_full = jnp.concatenate(parts, axis=0)
        d_half = d_full.astype(jnp.bfloat16)
        slab = slab_ref[by, pl.ds(bx * BLOCK, wide)].reshape(near, -1)
        g_ref[...] = lax.dot_general(
            d_half, slab, (((1,), (1,)), ((), ())), preferred_element_type=jnp.float32
        )
        d_turn = d_full.T.astype(jnp.bfloat16)
        turned = jnp.dot(d_turn, edge_ref[blk], preferred_element_type=jnp.float32)
        acc_ref[by, pl.ds(bx * BLOCK, wide)] += turned.T.reshape(wide, rows, -1)
        total = [jnp.zeros((own, 1), jnp.float32) for _ in range(3)]
        for c, w in chunks:
            nx, ny, nz, inv, q, p, s1, c1 = (field_ref[blk, n, :, c : c + w] for n in range(8))
            twice = 2.0 * c1
            s_before, s_now = jnp.zeros_like(s1), s1
            c_before, c_now = jnp.ones_like(c1), c1
            s_sum = [None] * 4
            c_sum = [None] * 4
            for b in range(nb):
                scaled = (b + 1.0) * c_now
                for m in range(4):
                    k = (b * 4 + m) * own
                    g = g_ref[k : k + own, c : c + w]
                    s_sum[m] = g * s_now if b == 0 else s_sum[m] + g * s_now
                    c_sum[m] = g * scaled if b == 0 else c_sum[m] + g * scaled
                s_before, s_now = s_now, twice * s_now - s_before
                c_before, c_now = c_now, twice * c_now - c_before
            s_dot = nx * s_sum[1] + ny * s_sum[2] + nz * s_sum[3]
            c_dot = nx * c_sum[1] + ny * c_sum[2] + nz * c_sum[3]
            slope = (q * (math.pi / CUTOFF)) * (c_sum[0] + root3 * c_dot) + p * (
                s_sum[0] + root3 * s_dot
            )
            across = root3 * q * inv
            along = slope - across * s_dot
            outs = [
                along * n + across * s_sum[m + 1] for m, n in enumerate((nx, ny, nz))
            ]
            for m in range(3):
                fj_ref[m : m + 1, c : c + w] = -jnp.sum(outs[m], axis=0, keepdims=True)
                total[m] = total[m] + jnp.sum(outs[m], axis=1, keepdims=True)
        for k in range(wide):
            wsum_ref[by, bx * BLOCK + k] += fj_ref[:, k * rows : (k + 1) * rows]
        lane = lax.broadcasted_iota(jnp.int32, (own, node_ref.shape[1]), 1)
        here = pl.ds(blk * own, own)
        node_ref[here] = jnp.where(
            lane == 0,
            total[0],
            jnp.where(lane == 1, total[1], jnp.where(lane == 2, total[2], en_ref[here])),
        )
        return carry

    lax.fori_loop(0, nbx * nby, backward, 0)

    def merge(x, carry):
        stack = jnp.concatenate([acc_ref[by, x] for by in range(nby)], axis=0)
        top = stack.astype(jnp.bfloat16)
        rest = (stack - top.astype(jnp.float32)).astype(jnp.bfloat16)
        fgrad_ref[x] = jnp.dot(
            pick_t_ref[...], top, preferred_element_type=jnp.float32
        ) + jnp.dot(pick_t_ref[...], rest, preferred_element_type=jnp.float32)
        return carry

    lax.fori_loop(0, px, merge, 0)


def ring(axis):
    count = lax.axis_size(axis)
    me = lax.axis_index(axis)
    return lax.rem(me + count - 1, count), lax.rem(me + 1, count)


def greet(around):
    barrier = pltpu.get_barrier_semaphore()
    for axis, sides in around.items():
        for side in sides:
            pl.semaphore_signal(
                barrier, inc=1, device_id={axis: side}, device_id_type=pl.DeviceIdType.MESH
            )
    return barrier


def sender(send_sem, recv_sem):
    def send(slot, source, target, axis, side):
        copy = pltpu.make_async_remote_copy(
            src_ref=source,
            dst_ref=target,
            send_sem=send_sem.at[slot],
            recv_sem=recv_sem.at[slot],
            device_id={axis: side},
            device_id_type=pl.DeviceIdType.MESH,
        )
        copy.start()
        return copy

    return send


def spread_kernel(
    dims,
    place_ref,
    feat_ref,
    small_ref,
    zsel_ref,
    ysel_ref,
    layer_ref,
    tile_ref,
    zs_ref,
    ys_ref,
    send_sem,
    recv_sem,
):
    sx, lat, reach, o, zp, yp = dims
    around = {axis: ring(axis) for axis in ("gz", "gy", "gx")}
    barrier = greet(around)
    send = sender(send_sem, recv_sem)
    tile_ref[0, 0, 0] = small_ref[...]
    for col in range(sx // lat):
        sites = jnp.dot(place_ref[col], feat_ref[col], preferred_element_type=jnp.float32)
        sites = sites.astype(jnp.bfloat16)
        for k in range(lat):
            x = col * lat + k
            own = sites[k * o : (k + 1) * o]
            layer_ref[reach + x, 0:o] = own
            faces = jnp.dot(zsel_ref[...], own, preferred_element_type=jnp.float32)
            faces = faces.astype(jnp.bfloat16)
            zs_ref[0, x] = faces[:zp]
            zs_ref[1, x] = faces[zp:]
    pl.semaphore_wait(barrier, 6)

    z0, y0 = o, o + 2 * zp
    inner = pl.ds(reach, sx)
    low, high = pl.ds(reach, reach), pl.ds(sx, reach)
    halo_low, halo_high = pl.ds(0, reach), pl.ds(reach + sx, reach)

    def send_x(slot, lanes, tiles):
        left, right = around["gx"]
        return [
            send(slot, layer_ref.at[low, lanes], layer_ref.at[halo_high, lanes], "gx", left),
            send(slot + 1, layer_ref.at[high, lanes], layer_ref.at[halo_low, lanes], "gx", right),
            send(slot + 2, tile_ref.at[(0,) + tiles], tile_ref.at[(2,) + tiles], "gx", left),
            send(slot + 3, tile_ref.at[(0,) + tiles], tile_ref.at[(1,) + tiles], "gx", right),
        ]

    left, right = around["gz"]
    z_copies = [
        send(0, zs_ref.at[0], layer_ref.at[inner, pl.ds(z0 + zp, zp)], "gz", left),
        send(1, zs_ref.at[1], layer_ref.at[inner, pl.ds(z0, zp)], "gz", right),
        send(2, tile_ref.at[0, 0, 0], tile_ref.at[0, 0, 2], "gz", left),
        send(3, tile_ref.at[0, 0, 0], tile_ref.at[0, 0, 1], "gz", right),
    ]
    x_copies = send_x(8, pl.ds(0, o), (0, 0))
    for copy in z_copies:
        copy.wait_recv()

    def faces_y(x, carry):
        faces = jnp.dot(ysel_ref[...], layer_ref[reach + x, 0:y0], preferred_element_type=jnp.float32)
        faces = faces.astype(jnp.bfloat16)
        ys_ref[0, x] = faces[:yp]
        ys_ref[1, x] = faces[yp:]
        return carry

    lax.fori_loop(0, sx, faces_y, 0)
    left, right = around["gy"]
    y_copies = [
        send(4, ys_ref.at[0], layer_ref.at[inner, pl.ds(y0 + yp, yp)], "gy", left),
        send(5, ys_ref.at[1], layer_ref.at[inner, pl.ds(y0, yp)], "gy", right),
        send(6, tile_ref.at[0, 0], tile_ref.at[0, 2], "gy", left),
        send(7, tile_ref.at[0, 0], tile_ref.at[0, 1], "gy", right),
    ]
    x_copies += send_x(12, pl.ds(z0, 2 * zp), (0, pl.ds(1, 2)))
    for copy in y_copies:
        copy.wait_recv()
    x_copies += send_x(16, pl.ds(y0, 2 * yp), (pl.ds(1, 2),))
    for copy in x_copies:
        copy.wait_recv()
    for copy in z_copies + y_copies + x_copies:
        copy.wait_send()


def gather_kernel(
    dims,
    place_ref,
    place_t_ref,
    grad_ref,
    force_ref,
    node_ref,
    zsel_ref,
    ysel_ref,
    out_ref,
    small_ref,
    sum_ref,
    fsum_ref,
    gs_ref,
    gr_ref,
    ys_ref,
    yr_ref,
    zs_ref,
    zr_ref,
    fr_ref,
    fyr_ref,
    fzr_ref,
    send_sem,
    recv_sem,
):
    sx, lat, reach, o, zp, yp = dims
    around = {axis: ring(axis) for axis in ("gz", "gy", "gx")}
    barrier = greet(around)
    send = sender(send_sem, recv_sem)
    z0, y0 = o, o + 2 * zp
    gs_ref[0] = grad_ref[0:reach].astype(jnp.bfloat16)
    gs_ref[1] = grad_ref[reach + sx : sx + 2 * reach].astype(jnp.bfloat16)
    sum_ref[...] = grad_ref[reach : reach + sx]
    pl.semaphore_wait(barrier, 6)

    left, right = around["gx"]
    pieces = [pl.ds(y0, 2 * yp), pl.ds(z0, 2 * zp), pl.ds(0, o)]
    x_copies = []
    for n, lanes in enumerate(pieces):
        for side, target in ((0, left), (1, right)):
            x_copies.append(
                send(
                    2 * n + side,
                    gs_ref.at[side, :, lanes],
                    gr_ref.at[side, :, lanes],
                    "gx",
                    target,
                )
            )
        if n == 0:
            f_copies = [
                send(6, force_ref.at[1], fr_ref.at[0], "gx", left),
                send(7, force_ref.at[2], fr_ref.at[1], "gx", right),
            ]

    def add_x(n, start, size):
        x_copies[2 * n].wait_recv()
        x_copies[2 * n + 1].wait_recv()
        rows = slice(start, start + size)
        sum_ref[sx - reach : sx, rows] += gr_ref[0, :, rows].astype(jnp.float32)
        sum_ref[0:reach, rows] += gr_ref[1, :, rows].astype(jnp.float32)

    add_x(0, y0, 2 * yp)
    ys_ref[0] = sum_ref[:, y0 : y0 + yp].astype(jnp.bfloat16)
    ys_ref[1] = sum_ref[:, y0 + yp : y0 + 2 * yp].astype(jnp.bfloat16)
    left, right = around["gy"]
    y_copies = [
        send(8, ys_ref.at[0], yr_ref.at[0], "gy", left),
        send(9, ys_ref.at[1], yr_ref.at[1], "gy", right),
    ]
    for copy in f_copies:
        copy.wait_recv()
    fsum_ref[...] = force_ref[0] + fr_ref[0] + fr_ref[1]
    fy_copies = [
        send(10, fsum_ref.at[1], fyr_ref.at[0], "gy", left),
        send(11, fsum_ref.at[2], fyr_ref.at[1], "gy", right),
    ]
    add_x(1, z0, 2 * zp)
    for copy in y_copies:
        copy.wait_recv()

    def add_y(x, carry):
        both = jnp.concatenate([yr_ref[1, x], yr_ref[0, x]], axis=0)
        sum_ref[x, 0:y0] += lax.dot_general(
            ysel_ref[...], both, (((0,), (0,)), ((), ())), preferred_element_type=jnp.float32
        )
        return carry

    lax.fori_loop(0, sx, add_y, 0)
    zs_ref[0] = sum_ref[:, z0 : z0 + zp].astype(jnp.bfloat16)
    zs_ref[1] = sum_ref[:, z0 + zp : z0 + 2 * zp].astype(jnp.bfloat16)
    zleft, zright = around["gz"]
    z_copies = [
        send(12, zs_ref.at[0], zr_ref.at[0], "gz", zleft),
        send(13, zs_ref.at[1], zr_ref.at[1], "gz", zright),
    ]
    for copy in fy_copies:
        copy.wait_recv()
    fsum_ref[0] += fyr_ref[0] + fyr_ref[1]
    fz_copies = [
        send(14, fsum_ref.at[0, 1], fzr_ref.at[0], "gz", zleft),
        send(15, fsum_ref.at[0, 2], fzr_ref.at[1], "gz", zright),
    ]
    add_x(2, 0, o)
    for copy in z_copies:
        copy.wait_recv()
    for copy in fz_copies:
        copy.wait_recv()
    tile = node_ref[...] + fsum_ref[0, 0] + fzr_ref[0] + fzr_ref[1]
    part = tile.shape[0] // (sx // lat)
    for col in range(sx // lat):
        sites = []
        for k in range(lat):
            x = col * lat + k
            both = jnp.concatenate([zr_ref[1, x], zr_ref[0, x]], axis=0)
            sites.append(
                sum_ref[x, 0:o]
                + lax.dot_general(
                    zsel_ref[...], both, (((0,), (0,)), ((), ())), preferred_element_type=jnp.float32
                )
            )
        whole = jnp.concatenate(sites, axis=0)
        top = whole.astype(jnp.bfloat16)
        rest = (whole - top.astype(jnp.float32)).astype(jnp.bfloat16)
        out_ref[col] = jnp.dot(
            place_t_ref[col], top, preferred_element_type=jnp.float32
        ) + jnp.dot(place_t_ref[col], rest, preferred_element_type=jnp.float32)
        small_ref[col] = jnp.dot(
            tile[col * part : (col + 1) * part],
            place_ref[col].astype(jnp.float32),
            precision=HIGH,
            preferred_element_type=jnp.float32,
        )
    for copy in x_copies + f_copies + y_copies + fy_copies + z_copies + fz_copies:
        copy.wait_send()


def tables(sx, sy, sz, reach):
    py, depth = sy + 2 * reach, sz + 2 * reach
    wide, nby = BLOCK + 2 * reach, sy // BLOCK
    up = lambda n: -(-n // 16) * 16
    o, zp, yp = sy * sz, up(sy * reach), up(reach * depth)
    z0, y0 = o, o + 2 * zp
    total = y0 + 2 * yp

    def row(y, z):
        if y < reach:
            return y0 + y * depth + z
        if y >= reach + sy:
            return y0 + yp + (y - reach - sy) * depth + z
        y -= reach
        if z < reach:
            return z0 + y * reach + z
        if z >= reach + sz:
            return z0 + zp + y * reach + z - reach - sz
        return y * sz + z - reach

    def spot(n, size):
        if n < reach:
            return 1, size - reach + n
        if n >= reach + size:
            return 2, n - reach - size
        return 0, n - reach

    pick = np.zeros((nby, wide, depth, total), np.float32)
    pick_pos = np.zeros((9 * o, nby, wide, depth), np.float32)
    for by in range(nby):
        for y in range(wide):
            for z in range(depth):
                pick[by, y, z, row(by * BLOCK + y, z)] = 1
                tile_y, at_y = spot(by * BLOCK + y, sy)
                tile_z, at_z = spot(z, sz)
                pick_pos[(tile_y * 3 + tile_z) * o + at_y * sz + at_z, by, y, z] = 1
    zsel = np.zeros((2, zp, o), np.float32)
    for y in range(sy):
        for k in range(reach):
            zsel[0, y * reach + k, y * sz + k] = 1
            zsel[1, y * reach + k, y * sz + sz - reach + k] = 1
    ysel = np.zeros((2, yp, y0), np.float32)
    for k in range(reach):
        for z in range(depth):
            ysel[0, k * depth + z, row(reach + k, z)] = 1
            ysel[1, k * depth + z, row(sy + k, z)] = 1
    return (
        (o, zp, yp, total),
        pick.reshape(-1, total),
        pick_pos.reshape(9 * o, -1),
        zsel.reshape(2 * zp, o),
        ysel.reshape(2 * yp, y0),
    )


def body(
    local_pos,
    counts,
    species,
    features,
    radial_weights,
    coupling,
    mixing,
    hidden_weights,
    output_weights,
):
    cx, cy, cz = counts.shape
    capacity, channels = features.shape[3:]
    nb = radial_weights.shape[1]
    lat, spacing, reach = lattice_of(capacity)
    sx, sy, sz = cx * lat, cy * lat, cz * lat
    nbx, nby = sx // BLOCK, sy // BLOCK
    wide, depth = BLOCK + 2 * reach, sz + 2 * reach
    near, own = wide * wide * depth, BLOCK * BLOCK * sz
    px, py = sx + 2 * reach, sy + 2 * reach
    rows = wide * depth
    blocks = nbx * nby
    (o, zp, yp, total), pick, pick_pos, zsel, ysel = tables(sx, sy, sz, reach)
    column = cy * cz * capacity

    occupied = (jnp.arange(capacity, dtype=jnp.int32) < counts[..., None]).astype(jnp.float32)
    site = jnp.clip(jnp.floor(local_pos * (1.0 / spacing)).astype(jnp.int32), 0, lat - 1)
    cell_y = np.arange(cy, dtype=np.int32)[None, :, None, None] * lat
    cell_z = np.arange(cz, dtype=np.int32)[None, None, :, None] * lat
    code = (site[:, :, :, 0] * sy + site[:, :, :, 1] + cell_y) * sz + site[:, :, :, 2] + cell_z
    code = code.reshape(cx, column)
    count = np.arange(column, dtype=np.int32)
    place = (code[:, None, :] == count[None, :, None]).astype(jnp.bfloat16)
    place_t = (code[:, :, None] == count[None, None, :]).astype(jnp.bfloat16)
    small = jnp.concatenate(
        [
            local_pos,
            occupied[:, :, :, None],
            species.astype(jnp.float32)[:, :, :, None],
        ],
        axis=3,
    )
    small = small.transpose(0, 3, 1, 2, 4).reshape(cx, 5, column)
    small_sites = jnp.einsum("xks,xst->xkt", small, place_t.astype(jnp.float32), precision=HIGH)

    vmem = pl.BlockSpec(memory_space=pltpu.VMEM)
    dims = (sx, lat, reach, o, zp, yp)
    limit = 50 * 1024 * 1024
    zsel_half = jnp.asarray(zsel, jnp.bfloat16)
    ysel_half = jnp.asarray(ysel, jnp.bfloat16)
    layers, tiles = pl.pallas_call(
        functools.partial(spread_kernel, dims),
        out_shape=(
            jax.ShapeDtypeStruct((px, total, channels), jnp.bfloat16),
            jax.ShapeDtypeStruct((3, 3, 3, cx * 4, lat * o), jnp.float32),
        ),
        in_specs=[vmem] * 5,
        out_specs=(vmem, vmem),
        scratch_shapes=[
            pltpu.VMEM((2, sx, zp, channels), jnp.bfloat16),
            pltpu.VMEM((2, sx, yp, channels), jnp.bfloat16),
            pltpu.SemaphoreType.DMA((20,)),
            pltpu.SemaphoreType.DMA((20,)),
        ],
        compiler_params=pltpu.CompilerParams(
            collective_id=0, has_side_effects=True, vmem_limit_bytes=limit
        ),
        name="halo_out",
    )(
        place,
        features.reshape(cx, column, channels),
        small_sites[:, :4].reshape(cx * 4, lat * o),
        zsel_half,
        ysel_half,
    )

    steps = [
        np.floor((np.arange(n) - reach) / lat).astype(np.float32) * SIDE
        for n in (px, py, depth)
    ]
    shifts = np.zeros((4, px, py, depth), np.float32)
    shifts[0] = steps[0][:, None, None]
    shifts[1] = steps[1][None, :, None]
    shifts[2] = steps[2][None, None, :]
    slab_shifts = np.stack(
        [shifts[:, :, by * BLOCK : by * BLOCK + wide].reshape(4, px, rows) for by in range(nby)]
    ).transpose(0, 2, 1, 3)
    order = (1, 0, 2)
    posw = jnp.stack([tiles[n] for n in order]).reshape(3, 9, cx, 4, lat, o)
    posw = posw.transpose(0, 2, 4, 3, 1, 5).reshape(3 * sx, 4, 9 * o)[sx - reach : 2 * sx + reach]
    posw = jnp.dot(posw.reshape(px * 4, 9 * o), jnp.asarray(pick_pos), precision=HIGH)
    posw = posw.reshape(px, 4, nby, rows).transpose(2, 0, 1, 3) + slab_shifts
    own_shift = np.concatenate(
        [
            shifts[:, reach : reach + sx, reach : reach + sy, reach : reach + sz],
            np.zeros((1, sx, sy, sz), np.float32),
        ]
    )
    small_grid = small_sites.reshape(cx, 5, lat, sy, sz).transpose(1, 0, 2, 3, 4).reshape(5, sx, sy, sz)
    rpos = (small_grid + own_shift).reshape(5, nbx, BLOCK, nby, BLOCK, sz)
    rpos = rpos.transpose(3, 1, 2, 4, 5, 0).reshape(blocks, own, 5)
    rpos = jnp.pad(rpos, ((0, 0), (0, 0), (0, 3)))

    spec_pad = -(-coupling.shape[1] // 8) * 8 - coupling.shape[1]
    total_own = sx * sy * sz
    pick_half = jnp.asarray(pick, jnp.bfloat16)
    fgrad, wsum, node = pl.pallas_call(
        functools.partial(compute_kernel, (sx, sy, sz, reach, nb)),
        out_shape=(
            jax.ShapeDtypeStruct((px, total, channels), jnp.float32),
            jax.ShapeDtypeStruct((nby, px, 4, rows), jnp.float32),
            jax.ShapeDtypeStruct((total_own, 128), jnp.float32),
        ),
        in_specs=[vmem] * 10,
        out_specs=(vmem, vmem, vmem),
        scratch_shapes=[
            pltpu.VMEM((blocks, 4, near), jnp.float32),
            pltpu.VMEM((4, near), jnp.float32),
            pltpu.VMEM((nby, px, rows, channels), jnp.bfloat16),
            pltpu.VMEM((blocks, nb * 4 * own, near), jnp.bfloat16),
            pltpu.VMEM((blocks, 8, own, near), jnp.float32),
            pltpu.VMEM((4, total_own, channels), jnp.float32),
            pltpu.VMEM((total_own, 128), jnp.float32),
            pltpu.VMEM((nby, px, rows, channels), jnp.float32),
            pltpu.VMEM((nb * 4 * own, near), jnp.float32),
        ],
        compiler_params=pltpu.CompilerParams(vmem_limit_bytes=limit),
        name="pair_layer",
    )(
        layers,
        posw,
        pick_half,
        jnp.asarray(pick.T, jnp.bfloat16),
        rpos,
        radial_weights,
        jnp.pad(coupling, ((0, 0), (0, spec_pad), (0, 0))),
        mixing,
        hidden_weights,
        output_weights[None, :],
    )

    force = wsum.transpose(1, 2, 0, 3).reshape(px * 4, nby * rows)
    force = jnp.dot(force, jnp.asarray(pick_pos.T), precision=HIGH).reshape(px, 4, 9 * o)
    force = jnp.pad(force, ((sx - reach, sx - reach), (0, 0), (0, 0)))
    force = force.reshape(3, cx, lat, 4, 9, o).transpose(0, 4, 1, 3, 2, 5)
    force = jnp.stack([force[n] for n in order]).reshape(3, 3, 3, cx * 4, lat * o)
    node = node[:, :4].reshape(nby, nbx, BLOCK, BLOCK, sz, 4)
    node = node.transpose(5, 1, 2, 0, 3, 4).reshape(4, cx, lat * o)
    node = node.transpose(1, 0, 2).reshape(cx * 4, lat * o)

    def half(*shape):
        return pltpu.VMEM(shape + (channels,), jnp.bfloat16)

    def tile(*lead):
        return pltpu.VMEM(lead + (cx * 4, lat * o), jnp.float32)

    grad, slots = pl.pallas_call(
        functools.partial(gather_kernel, dims),
        out_shape=(
            jax.ShapeDtypeStruct((cx, column, channels), jnp.float32),
            jax.ShapeDtypeStruct((cx, 4, column), jnp.float32),
        ),
        in_specs=[vmem] * 7,
        out_specs=(vmem, vmem),
        scratch_shapes=[
            pltpu.VMEM((sx, total, channels), jnp.float32),
            tile(3, 3),
            half(2, reach, total),
            half(2, reach, total),
            half(2, sx, yp),
            half(2, sx, yp),
            half(2, sx, zp),
            half(2, sx, zp),
            tile(2, 3, 3),
            tile(2, 3),
            tile(2),
            pltpu.SemaphoreType.DMA((16,)),
            pltpu.SemaphoreType.DMA((16,)),
        ],
        compiler_params=pltpu.CompilerParams(
            collective_id=1, has_side_effects=True, vmem_limit_bytes=limit
        ),
        name="halo_back",
    )(place, place_t, fgrad, force, node, zsel_half, ysel_half)
    slots = slots.reshape(cx, 4, cy, cz, capacity).transpose(0, 2, 3, 1, 4)
    return (
        slots[:, :, :, 3],
        slots[:, :, :, :3],
        grad.reshape(cx, cy, cz, capacity, channels),
    )


def solution(mesh):
    placed = (
        P("gx", "gy", "gz", None, None),
        P("gx", "gy", "gz"),
        P("gx", "gy", "gz", None),
        P("gx", "gy", "gz", None, None),
        P(),
        P(),
        P(),
        P(),
        P(),
    )
    return jax.shard_map(
        body,
        mesh=mesh,
        in_specs=placed,
        out_specs=(
            P("gx", "gy", "gz", None),
            P("gx", "gy", "gz", None, None),
            P("gx", "gy", "gz", None, None),
        ),
        check_vma=False,
    )
```

```python
import functools
import math

import jax
import jax.numpy as jnp
import numpy as np
from jax import lax
from jax.experimental import pallas as pl
from jax.experimental.pallas import tpu as pltpu
from jax.sharding import PartitionSpec as P

SIDE = 7.0
CUTOFF = 5.0
JITTER = 0.3
BLOCK = 2
HIGH = lax.Precision.HIGHEST


def lattice_of(capacity):
    lat = round(capacity ** (1.0 / 3.0))
    spacing = SIDE / lat
    reach = 0
    while (reach + 1 - 2 * JITTER) * spacing < CUTOFF:
        reach += 1
    return lat, spacing, reach


def pair_fields(pj, pi):
    dx = pj[0:1, :] - pi[:, 0:1]
    dy = pj[1:2, :] - pi[:, 1:2]
    dz = pj[2:3, :] - pi[:, 2:3]
    sq = dx * dx + dy * dy + dz * dz
    near = jnp.logical_and(sq < CUTOFF * CUTOFF, sq > 0.01)
    weight = jnp.where(near, pj[3:4, :] * pi[:, 3:4], 0.0)
    safe = jnp.where(near, sq, 1.0)
    inv = lax.rsqrt(safe)
    r = safe * inv
    u = r * (1.0 / CUTOFF)
    u2 = u * u
    u5 = u2 * u2 * u
    env = 1.0 + u5 * u * (-28.0 + u * (48.0 - 21.0 * u))
    denv = u5 * (-168.0 + u * (336.0 - 168.0 * u)) * (1.0 / CUTOFF)
    amp = weight * inv * math.sqrt(2.0 / CUTOFF)
    q = amp * env
    p = amp * denv - q * inv
    t = u * math.pi - 0.5 * math.pi
    t2 = t * t
    cos_t = 1.0 + t2 * (
        -1.0 / 2 + t2 * (1.0 / 24 + t2 * (-1.0 / 720 + t2 * (1.0 / 40320 + t2 * (-1.0 / 3628800 + t2 * (1.0 / 479001600)))))
    )
    sin_t = t * (
        1.0 + t2 * (-1.0 / 6 + t2 * (1.0 / 120 + t2 * (-1.0 / 5040 + t2 * (1.0 / 362880 + t2 * (-1.0 / 39916800)))))
    )
    return dx * inv, dy * inv, dz * inv, inv, q, p, cos_t, -sin_t


def compute_kernel(
    dims,
    layer_ref,
    posw_ref,
    pick_ref,
    pick_t_ref,
    rpos_ref,
    radial_ref,
    coupling_ref,
    mixing_ref,
    hw_ref,
    ow_ref,
    fgrad_ref,
    wsum_ref,
    node_ref,
    posj_ref,
    fj_ref,
    slab_ref,
    even_ref,
    odd_ref,
    field_ref,
    sv_ref,
    en_ref,
    acc_ref,
    geven_ref,
    godd_ref,
):
    sx, sy, sz, reach, nb = dims
    nbx, nby = sx // BLOCK, sy // BLOCK
    wide = BLOCK + 2 * reach
    depth = sz + 2 * reach
    rows = wide * depth
    near = wide * rows
    own = BLOCK * BLOCK * sz
    px = sx + 2 * reach
    chunks = [(c, min(128, near - c)) for c in range(0, near, 128)]
    root3 = math.sqrt(3.0)

    for x in range(px):
        full = jnp.dot(pick_ref[...], layer_ref[x], preferred_element_type=jnp.float32)
        full = full.astype(jnp.bfloat16)
        for by in range(nby):
            slab_ref[by, x] = full[by * rows : (by + 1) * rows]
            acc_ref[by, x] = jnp.zeros((rows, full.shape[1]), jnp.float32)
    wsum_ref[...] = jnp.zeros(wsum_ref.shape, jnp.float32)
    fj_ref[...] = jnp.zeros(fj_ref.shape, jnp.float32)

    for by in range(nby):
        for bx in range(nbx):
            for k in range(wide):
                posj_ref[by * nbx + bx, :, k * rows : (k + 1) * rows] = posw_ref[by, bx * BLOCK + k]

    blocks = nbx * nby
    half = blocks // 2

    def basis(blk, edge_ref, slot):
        pi = rpos_ref[blk]
        for c, w in chunks:
            pj = posj_ref[blk, :, c : c + w]
            nx, ny, nz, inv, q, p, s1, c1 = pair_fields(pj, pi)
            field_ref[blk, 0, :, c : c + w] = nx
            field_ref[blk, 1, :, c : c + w] = ny
            field_ref[blk, 2, :, c : c + w] = nz
            field_ref[blk, 3, :, c : c + w] = inv
            field_ref[blk, 4, :, c : c + w] = q
            field_ref[blk, 5, :, c : c + w] = p
            field_ref[blk, 6, :, c : c + w] = s1
            field_ref[blk, 7, :, c : c + w] = c1
            twice = 2.0 * c1
            before, now = jnp.zeros_like(s1), s1
            q3 = root3 * q
            qs = (q, q3 * nx, q3 * ny, q3 * nz)
            for b in range(nb):
                for m in range(4):
                    k = (b * 4 + m) * own
                    edge_ref[slot, k : k + own, c : c + w] = (qs[m] * now).astype(jnp.bfloat16)
                before, now = now, twice * now - before

    def gather(blk, edge_ref, slot):
        by, bx = blk // nbx, lax.rem(blk, nbx)
        slab = slab_ref[by, pl.ds(bx * BLOCK, wide)].reshape(near, -1)
        summed = jnp.dot(edge_ref[slot], slab, preferred_element_type=jnp.float32)
        for m in range(4):
            total = None
            for b in range(nb):
                k = (b * 4 + m) * own
                term = summed[k : k + own] * radial_ref[min(m, 1), b : b + 1, :]
                total = term if total is None else total + term
            sv_ref[m, pl.ds(blk * own, own)] = total

    def forward(i, carry):
        gather(2 * i, even_ref, i)
        basis(2 * i + 1, odd_ref, i)
        gather(2 * i + 1, odd_ref, i)
        basis(2 * i + 2, even_ref, i + 1)
        return carry

    basis(0, even_ref, 0)
    lax.fori_loop(0, half - 1, forward, 0)
    gather(blocks - 2, even_ref, half - 1)
    basis(blocks - 1, odd_ref, half - 1)
    gather(blocks - 1, odd_ref, half - 1)

    flat = rpos_ref[...].reshape(nbx * nby * own, -1)
    occ = flat[:, 3:4]
    kind = flat[:, 4:5]
    spec = lax.broadcasted_iota(jnp.int32, (flat.shape[0], coupling_ref.shape[1]), 1)
    onehot = (kind.astype(jnp.int32) == spec).astype(jnp.float32)
    wq = [
        jnp.dot(onehot, coupling_ref[n], precision=HIGH, preferred_element_type=jnp.float32)
        for n in range(3)
    ]
    scalar = sv_ref[0]
    length_sq = sv_ref[1] * sv_ref[1] + sv_ref[2] * sv_ref[2] + sv_ref[3] * sv_ref[3]
    product = wq[0] * scalar + wq[1] * scalar * scalar + wq[2] * length_sq
    fold = jnp.dot(mixing_ref[...], hw_ref[...], precision=HIGH, preferred_element_type=jnp.float32)
    hidden = jnp.dot(product, fold, precision=HIGH, preferred_element_type=jnp.float32)
    logistic = jax.nn.sigmoid(hidden)
    energy = occ * jnp.sum(ow_ref[...] * hidden * logistic, axis=1, keepdims=True)
    d_hidden = occ * ow_ref[...] * logistic * (1.0 + hidden * (1.0 - logistic))
    d_product = lax.dot_general(
        d_hidden, fold, (((1,), (1,)), ((), ())), precision=HIGH, preferred_element_type=jnp.float32
    )
    en_ref[...] = jnp.broadcast_to(energy, en_ref.shape)
    sv_ref[0] = d_product * (wq[0] + 2.0 * wq[1] * scalar)
    twice_d = 2.0 * wq[2] * d_product
    for m in range(1, 4):
        sv_ref[m] = twice_d * sv_ref[m]

    def scatter(blk, edge_ref, slot, g_ref):
        by, bx = blk // nbx, lax.rem(blk, nbx)
        parts = []
        for b in range(nb):
            for m in range(4):
                parts.append(
                    sv_ref[m, pl.ds(blk * own, own)] * radial_ref[min(m, 1), b : b + 1, :]
                )
        d_full = jnp.concatenate(parts, axis=0)
        d_half = d_full.astype(jnp.bfloat16)
        slab = slab_ref[by, pl.ds(bx * BLOCK, wide)].reshape(near, -1)
        g_ref[...] = lax.dot_general(
            d_half, slab, (((1,), (1,)), ((), ())), preferred_element_type=jnp.float32
        )
        d_turn = d_full.T.astype(jnp.bfloat16)
        turned = jnp.dot(d_turn, edge_ref[slot], preferred_element_type=jnp.float32)
        acc_ref[by, pl.ds(bx * BLOCK, wide)] += turned.T.reshape(wide, rows, -1)

    def forces(blk, g_ref):
        by, bx = blk // nbx, lax.rem(blk, nbx)
        total = [jnp.zeros((own, 1), jnp.float32) for _ in range(3)]
        for c, w in chunks:
            nx, ny, nz, inv, q, p, s1, c1 = (field_ref[blk, n, :, c : c + w] for n in range(8))
            twice = 2.0 * c1
            s_before, s_now = jnp.zeros_like(s1), s1
            c_before, c_now = jnp.ones_like(c1), c1
            s_sum = [None] * 4
            c_sum = [None] * 4
            for b in range(nb):
                scaled = (b + 1.0) * c_now
                for m in range(4):
                    k = (b * 4 + m) * own
                    g = g_ref[k : k + own, c : c + w]
                    s_sum[m] = g * s_now if b == 0 else s_sum[m] + g * s_now
                    c_sum[m] = g * scaled if b == 0 else c_sum[m] + g * scaled
                s_before, s_now = s_now, twice * s_now - s_before
                c_before, c_now = c_now, twice * c_now - c_before
            s_dot = nx * s_sum[1] + ny * s_sum[2] + nz * s_sum[3]
            c_dot = nx * c_sum[1] + ny * c_sum[2] + nz * c_sum[3]
            slope = (q * (math.pi / CUTOFF)) * (c_sum[0] + root3 * c_dot) + p * (
                s_sum[0] + root3 * s_dot
            )
            across = root3 * q * inv
            along = slope - across * s_dot
            outs = [
                along * n + across * s_sum[m + 1] for m, n in enumerate((nx, ny, nz))
            ]
            for m in range(3):
                fj_ref[m : m + 1, c : c + w] = -jnp.sum(outs[m], axis=0, keepdims=True)
                total[m] = total[m] + jnp.sum(outs[m], axis=1, keepdims=True)
        for k in range(wide):
            wsum_ref[by, bx * BLOCK + k] += fj_ref[:, k * rows : (k + 1) * rows]
        lane = lax.broadcasted_iota(jnp.int32, (own, node_ref.shape[1]), 1)
        here = pl.ds(blk * own, own)
        node_ref[here] = jnp.where(
            lane == 0,
            total[0],
            jnp.where(lane == 1, total[1], jnp.where(lane == 2, total[2], en_ref[here])),
        )

    def backward(i, carry):
        scatter(2 * i + 1, odd_ref, i, godd_ref)
        forces(2 * i, geven_ref)
        scatter(2 * i + 2, even_ref, i + 1, geven_ref)
        forces(2 * i + 1, godd_ref)
        return carry

    scatter(0, even_ref, 0, geven_ref)
    lax.fori_loop(0, half - 1, backward, 0)
    scatter(blocks - 1, odd_ref, half - 1, godd_ref)
    forces(blocks - 2, geven_ref)
    forces(blocks - 1, godd_ref)

    for x in range(px):
        stack = jnp.concatenate([acc_ref[by, x] for by in range(nby)], axis=0)
        top = stack.astype(jnp.bfloat16)
        rest = (stack - top.astype(jnp.float32)).astype(jnp.bfloat16)
        fgrad_ref[x] = jnp.dot(
            pick_t_ref[...], top, preferred_element_type=jnp.float32
        ) + jnp.dot(pick_t_ref[...], rest, preferred_element_type=jnp.float32)


def ring(axis):
    count = lax.axis_size(axis)
    me = lax.axis_index(axis)
    return lax.rem(me + count - 1, count), lax.rem(me + 1, count)


def greet(around):
    barrier = pltpu.get_barrier_semaphore()
    for axis, sides in around.items():
        for side in sides:
            pl.semaphore_signal(
                barrier, inc=1, device_id={axis: side}, device_id_type=pl.DeviceIdType.MESH
            )
    return barrier


def sender(send_sem, recv_sem):
    def send(slot, source, target, axis, side):
        copy = pltpu.make_async_remote_copy(
            src_ref=source,
            dst_ref=target,
            send_sem=send_sem.at[slot],
            recv_sem=recv_sem.at[slot],
            device_id={axis: side},
            device_id_type=pl.DeviceIdType.MESH,
        )
        copy.start()
        return copy

    return send


def spread_kernel(
    dims,
    spacing,
    counts_ref,
    pos_ref,
    kind_ref,
    feat_ref,
    zsel_ref,
    ysel_ref,
    layer_ref,
    tile_ref,
    place_ref,
    small_ref,
    zs_ref,
    ys_ref,
    send_sem,
    recv_sem,
):
    sx, lat, reach, o, zp, yp = dims
    around = {axis: ring(axis) for axis in ("gz", "gy", "gx")}
    barrier = greet(around)
    send = sender(send_sem, recv_sem)
    cx, cy, cz, _, capacity = pos_ref.shape
    sy, sz = cy * lat, cz * lat
    slot = lax.broadcasted_iota(jnp.int32, (1, capacity), 1)
    for col in range(cx):
        pieces, codes = [], []
        for cell_y in range(cy):
            for cell_z in range(cz):
                xyz = pos_ref[col, cell_y, cell_z]
                site = jnp.clip(jnp.floor(xyz * (1.0 / spacing)), 0.0, lat - 1.0)
                codes.append(
                    (site[0:1] * sy + site[1:2] + cell_y * lat) * sz + site[2:3] + cell_z * lat
                )
                occ = (slot < counts_ref[col, cell_y, cell_z]).astype(jnp.float32)
                kind = kind_ref[col, cell_y, cell_z : cell_z + 1].astype(jnp.float32)
                pieces.append(
                    jnp.concatenate([xyz, occ, kind, jnp.zeros((3, capacity), jnp.float32)], axis=0)
                )
        code = jnp.concatenate(codes, axis=1)
        small = jnp.concatenate(pieces, axis=1)
        count = code.shape[1]
        place = (
            code == lax.broadcasted_iota(jnp.int32, (count, count), 0).astype(jnp.float32)
        ).astype(jnp.float32)
        small = lax.dot_general(
            small, place, (((1,), (1,)), ((), ())), precision=HIGH, preferred_element_type=jnp.float32
        )
        small_ref[col] = small
        tile_ref[0, 0, 0, col * 4 : (col + 1) * 4] = small[0:4]
        place_ref[col] = place.astype(jnp.bfloat16)
        sites = jnp.dot(place_ref[col], feat_ref[col], preferred_element_type=jnp.float32)
        sites = sites.astype(jnp.bfloat16)
        for k in range(lat):
            x = col * lat + k
            own = sites[k * o : (k + 1) * o]
            layer_ref[reach + x, 0:o] = own
            faces = jnp.dot(zsel_ref[...], own, preferred_element_type=jnp.float32)
            faces = faces.astype(jnp.bfloat16)
            zs_ref[0, x] = faces[:zp]
            zs_ref[1, x] = faces[zp:]
    pl.semaphore_wait(barrier, 6)

    z0, y0 = o, o + 2 * zp
    inner = pl.ds(reach, sx)
    low, high = pl.ds(reach, reach), pl.ds(sx, reach)
    halo_low, halo_high = pl.ds(0, reach), pl.ds(reach + sx, reach)

    def send_x(slot, lanes, tiles):
        left, right = around["gx"]
        return [
            send(slot, layer_ref.at[low, lanes], layer_ref.at[halo_high, lanes], "gx", left),
            send(slot + 1, layer_ref.at[high, lanes], layer_ref.at[halo_low, lanes], "gx", right),
            send(slot + 2, tile_ref.at[(0,) + tiles], tile_ref.at[(2,) + tiles], "gx", left),
            send(slot + 3, tile_ref.at[(0,) + tiles], tile_ref.at[(1,) + tiles], "gx", right),
        ]

    left, right = around["gz"]
    z_copies = [
        send(0, zs_ref.at[0], layer_ref.at[inner, pl.ds(z0 + zp, zp)], "gz", left),
        send(1, zs_ref.at[1], layer_ref.at[inner, pl.ds(z0, zp)], "gz", right),
        send(2, tile_ref.at[0, 0, 0], tile_ref.at[0, 0, 2], "gz", left),
        send(3, tile_ref.at[0, 0, 0], tile_ref.at[0, 0, 1], "gz", right),
    ]
    x_copies = send_x(8, pl.ds(0, o), (0, 0))
    for copy in z_copies:
        copy.wait_recv()

    def faces_y(x, carry):
        faces = jnp.dot(ysel_ref[...], layer_ref[reach + x, 0:y0], preferred_element_type=jnp.float32)
        faces = faces.astype(jnp.bfloat16)
        ys_ref[0, x] = faces[:yp]
        ys_ref[1, x] = faces[yp:]
        return carry

    lax.fori_loop(0, sx, faces_y, 0)
    left, right = around["gy"]
    y_copies = [
        send(4, ys_ref.at[0], layer_ref.at[inner, pl.ds(y0 + yp, yp)], "gy", left),
        send(5, ys_ref.at[1], layer_ref.at[inner, pl.ds(y0, yp)], "gy", right),
        send(6, tile_ref.at[0, 0], tile_ref.at[0, 2], "gy", left),
        send(7, tile_ref.at[0, 0], tile_ref.at[0, 1], "gy", right),
    ]
    x_copies += send_x(12, pl.ds(z0, 2 * zp), (0, pl.ds(1, 2)))
    for copy in y_copies:
        copy.wait_recv()
    x_copies += send_x(16, pl.ds(y0, 2 * yp), (pl.ds(1, 2),))
    for copy in x_copies:
        copy.wait_recv()
    for copy in z_copies + y_copies + x_copies:
        copy.wait_send()


def gather_kernel(
    dims,
    place_ref,
    grad_ref,
    force_ref,
    node_ref,
    zsel_ref,
    ysel_ref,
    out_ref,
    energy_ref,
    xyz_ref,
    sum_ref,
    fsum_ref,
    gs_ref,
    gr_ref,
    ys_ref,
    yr_ref,
    zs_ref,
    zr_ref,
    fr_ref,
    fyr_ref,
    fzr_ref,
    send_sem,
    recv_sem,
):
    sx, lat, reach, o, zp, yp = dims
    around = {axis: ring(axis) for axis in ("gz", "gy", "gx")}
    barrier = greet(around)
    send = sender(send_sem, recv_sem)
    z0, y0 = o, o + 2 * zp
    gs_ref[0] = grad_ref[0:reach].astype(jnp.bfloat16)
    gs_ref[1] = grad_ref[reach + sx : sx + 2 * reach].astype(jnp.bfloat16)
    sum_ref[...] = grad_ref[reach : reach + sx]
    pl.semaphore_wait(barrier, 6)

    left, right = around["gx"]
    pieces = [pl.ds(y0, 2 * yp), pl.ds(z0, 2 * zp), pl.ds(0, o)]
    x_copies = []
    for n, lanes in enumerate(pieces):
        for side, target in ((0, left), (1, right)):
            x_copies.append(
                send(
                    2 * n + side,
                    gs_ref.at[side, :, lanes],
                    gr_ref.at[side, :, lanes],
                    "gx",
                    target,
                )
            )
        if n == 0:
            f_copies = [
                send(6, force_ref.at[1], fr_ref.at[0], "gx", left),
                send(7, force_ref.at[2], fr_ref.at[1], "gx", right),
            ]

    def add_x(n, start, size):
        x_copies[2 * n].wait_recv()
        x_copies[2 * n + 1].wait_recv()
        rows = slice(start, start + size)
        sum_ref[sx - reach : sx, rows] += gr_ref[0, :, rows].astype(jnp.float32)
        sum_ref[0:reach, rows] += gr_ref[1, :, rows].astype(jnp.float32)

    add_x(0, y0, 2 * yp)
    ys_ref[0] = sum_ref[:, y0 : y0 + yp].astype(jnp.bfloat16)
    ys_ref[1] = sum_ref[:, y0 + yp : y0 + 2 * yp].astype(jnp.bfloat16)
    left, right = around["gy"]
    y_copies = [
        send(8, ys_ref.at[0], yr_ref.at[0], "gy", left),
        send(9, ys_ref.at[1], yr_ref.at[1], "gy", right),
    ]
    for copy in f_copies:
        copy.wait_recv()
    fsum_ref[...] = force_ref[0] + fr_ref[0] + fr_ref[1]
    fy_copies = [
        send(10, fsum_ref.at[1], fyr_ref.at[0], "gy", left),
        send(11, fsum_ref.at[2], fyr_ref.at[1], "gy", right),
    ]
    add_x(1, z0, 2 * zp)
    for copy in y_copies:
        copy.wait_recv()

    def add_y(x, carry):
        both = jnp.concatenate([yr_ref[1, x], yr_ref[0, x]], axis=0)
        sum_ref[x, 0:y0] += lax.dot_general(
            ysel_ref[...], both, (((0,), (0,)), ((), ())), preferred_element_type=jnp.float32
        )
        return carry

    lax.fori_loop(0, sx, add_y, 0)
    zs_ref[0] = sum_ref[:, z0 : z0 + zp].astype(jnp.bfloat16)
    zs_ref[1] = sum_ref[:, z0 + zp : z0 + 2 * zp].astype(jnp.bfloat16)
    zleft, zright = around["gz"]
    z_copies = [
        send(12, zs_ref.at[0], zr_ref.at[0], "gz", zleft),
        send(13, zs_ref.at[1], zr_ref.at[1], "gz", zright),
    ]
    for copy in fy_copies:
        copy.wait_recv()
    fsum_ref[0] += fyr_ref[0] + fyr_ref[1]
    fz_copies = [
        send(14, fsum_ref.at[0, 1], fzr_ref.at[0], "gz", zleft),
        send(15, fsum_ref.at[0, 2], fzr_ref.at[1], "gz", zright),
    ]
    add_x(2, 0, o)
    for copy in z_copies:
        copy.wait_recv()
    for copy in fz_copies:
        copy.wait_recv()
    tile = node_ref[...] + fsum_ref[0, 0] + fzr_ref[0] + fzr_ref[1]
    part = tile.shape[0] // (sx // lat)
    for col in range(sx // lat):
        sites = []
        for k in range(lat):
            x = col * lat + k
            both = jnp.concatenate([zr_ref[1, x], zr_ref[0, x]], axis=0)
            sites.append(
                sum_ref[x, 0:o]
                + lax.dot_general(
                    zsel_ref[...], both, (((0,), (0,)), ((), ())), preferred_element_type=jnp.float32
                )
            )
        whole = jnp.concatenate(sites, axis=0)
        top = whole.astype(jnp.bfloat16)
        rest = (whole - top.astype(jnp.float32)).astype(jnp.bfloat16)
        turn = place_ref[col].astype(jnp.float32).T.astype(jnp.bfloat16)
        out_ref[col] = jnp.dot(turn, top, preferred_element_type=jnp.float32) + jnp.dot(
            turn, rest, preferred_element_type=jnp.float32
        )
        slots = jnp.dot(
            tile[col * part : (col + 1) * part],
            place_ref[col].astype(jnp.float32),
            precision=HIGH,
            preferred_element_type=jnp.float32,
        )
        _, cy, cz, _, capacity = xyz_ref.shape
        for n in range(cy * cz):
            lanes = slice(n * capacity, (n + 1) * capacity)
            xyz_ref[col, n // cz, n % cz] = slots[0:3, lanes]
            energy_ref[col, n // cz, n % cz : n % cz + 1] = slots[3:4, lanes]
    for copy in x_copies + f_copies + y_copies + fy_copies + z_copies + fz_copies:
        copy.wait_send()


def tables(sx, sy, sz, reach):
    py, depth = sy + 2 * reach, sz + 2 * reach
    wide, nby = BLOCK + 2 * reach, sy // BLOCK
    up = lambda n: -(-n // 16) * 16
    o, zp, yp = sy * sz, up(sy * reach), up(reach * depth)
    z0, y0 = o, o + 2 * zp
    total = y0 + 2 * yp

    def row(y, z):
        if y < reach:
            return y0 + y * depth + z
        if y >= reach + sy:
            return y0 + yp + (y - reach - sy) * depth + z
        y -= reach
        if z < reach:
            return z0 + y * reach + z
        if z >= reach + sz:
            return z0 + zp + y * reach + z - reach - sz
        return y * sz + z - reach

    def spot(n, size):
        if n < reach:
            return 1, size - reach + n
        if n >= reach + size:
            return 2, n - reach - size
        return 0, n - reach

    pick = np.zeros((nby, wide, depth, total), np.float32)
    pick_pos = np.zeros((9 * o, nby, wide, depth), np.float32)
    for by in range(nby):
        for y in range(wide):
            for z in range(depth):
                pick[by, y, z, row(by * BLOCK + y, z)] = 1
                tile_y, at_y = spot(by * BLOCK + y, sy)
                tile_z, at_z = spot(z, sz)
                pick_pos[(tile_y * 3 + tile_z) * o + at_y * sz + at_z, by, y, z] = 1
    zsel = np.zeros((2, zp, o), np.float32)
    for y in range(sy):
        for k in range(reach):
            zsel[0, y * reach + k, y * sz + k] = 1
            zsel[1, y * reach + k, y * sz + sz - reach + k] = 1
    ysel = np.zeros((2, yp, y0), np.float32)
    for k in range(reach):
        for z in range(depth):
            ysel[0, k * depth + z, row(reach + k, z)] = 1
            ysel[1, k * depth + z, row(sy + k, z)] = 1
    return (
        (o, zp, yp, total),
        pick.reshape(-1, total),
        pick_pos.reshape(9 * o, -1),
        zsel.reshape(2 * zp, o),
        ysel.reshape(2 * yp, y0),
    )


def body(
    local_pos,
    counts,
    species,
    features,
    radial_weights,
    coupling,
    mixing,
    hidden_weights,
    output_weights,
):
    cx, cy, cz = counts.shape
    capacity, channels = features.shape[3:]
    nb = radial_weights.shape[1]
    lat, spacing, reach = lattice_of(capacity)
    sx, sy, sz = cx * lat, cy * lat, cz * lat
    nbx, nby = sx // BLOCK, sy // BLOCK
    wide, depth = BLOCK + 2 * reach, sz + 2 * reach
    near, own = wide * wide * depth, BLOCK * BLOCK * sz
    px, py = sx + 2 * reach, sy + 2 * reach
    rows = wide * depth
    blocks = nbx * nby
    (o, zp, yp, total), pick, pick_pos, zsel, ysel = tables(sx, sy, sz, reach)
    column = cy * cz * capacity

    vmem = pl.BlockSpec(memory_space=pltpu.VMEM)
    dims = (sx, lat, reach, o, zp, yp)
    limit = 50 * 1024 * 1024
    zsel_half = jnp.asarray(zsel, jnp.bfloat16)
    ysel_half = jnp.asarray(ysel, jnp.bfloat16)
    layers, tiles, place, small_sites = pl.pallas_call(
        functools.partial(spread_kernel, dims, spacing),
        out_shape=(
            jax.ShapeDtypeStruct((px, total, channels), jnp.bfloat16),
            jax.ShapeDtypeStruct((3, 3, 3, cx * 4, lat * o), jnp.float32),
            jax.ShapeDtypeStruct((cx, column, column), jnp.bfloat16),
            jax.ShapeDtypeStruct((cx, 8, column), jnp.float32),
        ),
        in_specs=[pl.BlockSpec(memory_space=pltpu.SMEM)] + [vmem] * 5,
        out_specs=(vmem,) * 4,
        scratch_shapes=[
            pltpu.VMEM((2, sx, zp, channels), jnp.bfloat16),
            pltpu.VMEM((2, sx, yp, channels), jnp.bfloat16),
            pltpu.SemaphoreType.DMA((20,)),
            pltpu.SemaphoreType.DMA((20,)),
        ],
        compiler_params=pltpu.CompilerParams(
            collective_id=0, has_side_effects=True, vmem_limit_bytes=limit
        ),
        name="halo_out",
    )(
        counts,
        local_pos,
        species,
        features.reshape(cx, column, channels),
        zsel_half,
        ysel_half,
    )

    steps = [
        np.floor((np.arange(n) - reach) / lat).astype(np.float32) * SIDE
        for n in (px, py, depth)
    ]
    shifts = np.zeros((4, px, py, depth), np.float32)
    shifts[0] = steps[0][:, None, None]
    shifts[1] = steps[1][None, :, None]
    shifts[2] = steps[2][None, None, :]
    slab_shifts = np.stack(
        [shifts[:, :, by * BLOCK : by * BLOCK + wide].reshape(4, px, rows) for by in range(nby)]
    ).transpose(0, 2, 1, 3)
    order = (1, 0, 2)
    posw = jnp.stack([tiles[n] for n in order]).reshape(3, 9, cx, 4, lat, o)
    posw = posw.transpose(0, 2, 4, 3, 1, 5).reshape(3 * sx, 4, 9 * o)[sx - reach : 2 * sx + reach]
    posw = jnp.dot(posw.reshape(px * 4, 9 * o), jnp.asarray(pick_pos), precision=HIGH)
    posw = posw.reshape(px, 4, nby, rows).transpose(2, 0, 1, 3) + slab_shifts
    own_shift = np.concatenate(
        [
            shifts[:, reach : reach + sx, reach : reach + sy, reach : reach + sz],
            np.zeros((1, sx, sy, sz), np.float32),
        ]
    )
    small_grid = small_sites[:, :5].reshape(cx, 5, lat, sy, sz).transpose(1, 0, 2, 3, 4).reshape(5, sx, sy, sz)
    rpos = (small_grid + own_shift).reshape(5, nbx, BLOCK, nby, BLOCK, sz)
    rpos = rpos.transpose(3, 1, 2, 4, 5, 0).reshape(blocks, own, 5)
    rpos = jnp.pad(rpos, ((0, 0), (0, 0), (0, 3)))

    spec_pad = -(-coupling.shape[1] // 8) * 8 - coupling.shape[1]
    total_own = sx * sy * sz
    pick_half = jnp.asarray(pick, jnp.bfloat16)
    fgrad, wsum, node = pl.pallas_call(
        functools.partial(compute_kernel, (sx, sy, sz, reach, nb)),
        out_shape=(
            jax.ShapeDtypeStruct((px, total, channels), jnp.float32),
            jax.ShapeDtypeStruct((nby, px, 4, rows), jnp.float32),
            jax.ShapeDtypeStruct((total_own, 128), jnp.float32),
        ),
        in_specs=[vmem] * 10,
        out_specs=(vmem, vmem, vmem),
        scratch_shapes=[
            pltpu.VMEM((blocks, 4, near), jnp.float32),
            pltpu.VMEM((4, near), jnp.float32),
            pltpu.VMEM((nby, px, rows, channels), jnp.bfloat16),
            pltpu.VMEM((blocks // 2, nb * 4 * own, near), jnp.bfloat16),
            pltpu.VMEM((blocks // 2, nb * 4 * own, near), jnp.bfloat16),
            pltpu.VMEM((blocks, 8, own, near), jnp.float32),
            pltpu.VMEM((4, total_own, channels), jnp.float32),
            pltpu.VMEM((total_own, 128), jnp.float32),
            pltpu.VMEM((nby, px, rows, channels), jnp.float32),
            pltpu.VMEM((nb * 4 * own, near), jnp.float32),
            pltpu.VMEM((nb * 4 * own, near), jnp.float32),
        ],
        compiler_params=pltpu.CompilerParams(vmem_limit_bytes=limit),
        name="pair_layer",
    )(
        layers,
        posw,
        pick_half,
        jnp.asarray(pick.T, jnp.bfloat16),
        rpos,
        radial_weights,
        jnp.pad(coupling, ((0, 0), (0, spec_pad), (0, 0))),
        mixing,
        hidden_weights,
        output_weights[None, :],
    )

    force = wsum.transpose(1, 2, 0, 3).reshape(px * 4, nby * rows)
    force = jnp.dot(force, jnp.asarray(pick_pos.T), precision=HIGH).reshape(px, 4, 9 * o)
    force = jnp.pad(force, ((sx - reach, sx - reach), (0, 0), (0, 0)))
    force = force.reshape(3, cx, lat, 4, 9, o).transpose(0, 4, 1, 3, 2, 5)
    force = jnp.stack([force[n] for n in order]).reshape(3, 3, 3, cx * 4, lat * o)
    node = node[:, :4].reshape(nby, nbx, BLOCK, BLOCK, sz, 4)
    node = node.transpose(5, 1, 2, 0, 3, 4).reshape(4, cx, lat * o)
    node = node.transpose(1, 0, 2).reshape(cx * 4, lat * o)

    def half(*shape):
        return pltpu.VMEM(shape + (channels,), jnp.bfloat16)

    def tile(*lead):
        return pltpu.VMEM(lead + (cx * 4, lat * o), jnp.float32)

    grad, energy, forces = pl.pallas_call(
        functools.partial(gather_kernel, dims),
        out_shape=(
            jax.ShapeDtypeStruct((cx, column, channels), jnp.float32),
            jax.ShapeDtypeStruct((cx, cy, cz, capacity), jnp.float32),
            jax.ShapeDtypeStruct((cx, cy, cz, 3, capacity), jnp.float32),
        ),
        in_specs=[vmem] * 6,
        out_specs=(vmem, vmem, vmem),
        scratch_shapes=[
            pltpu.VMEM((sx, total, channels), jnp.float32),
            tile(3, 3),
            half(2, reach, total),
            half(2, reach, total),
            half(2, sx, yp),
            half(2, sx, yp),
            half(2, sx, zp),
            half(2, sx, zp),
            tile(2, 3, 3),
            tile(2, 3),
            tile(2),
            pltpu.SemaphoreType.DMA((16,)),
            pltpu.SemaphoreType.DMA((16,)),
        ],
        compiler_params=pltpu.CompilerParams(
            collective_id=1, has_side_effects=True, vmem_limit_bytes=limit
        ),
        name="halo_back",
    )(place, fgrad, force, node, zsel_half, ysel_half)
    return energy, forces, grad.reshape(cx, cy, cz, capacity, channels)


def solution(mesh):
    placed = (
        P("gx", "gy", "gz", None, None),
        P("gx", "gy", "gz"),
        P("gx", "gy", "gz", None),
        P("gx", "gy", "gz", None, None),
        P(),
        P(),
        P(),
        P(),
        P(),
    )
    return jax.shard_map(
        body,
        mesh=mesh,
        in_specs=placed,
        out_specs=(
            P("gx", "gy", "gz", None),
            P("gx", "gy", "gz", None, None),
            P("gx", "gy", "gz", None, None),
        ),
        check_vma=False,
    )
```

```python
import functools
import math

import jax
import jax.numpy as jnp
import numpy as np
from jax import lax
from jax.experimental import pallas as pl
from jax.experimental.pallas import tpu as pltpu
from jax.sharding import PartitionSpec as P

SIDE = 7.0
CUTOFF = 5.0
JITTER = 0.3
BLOCK = 2
HIGH = lax.Precision.HIGHEST


def lattice_of(capacity):
    lat = round(capacity ** (1.0 / 3.0))
    spacing = SIDE / lat
    reach = 0
    while (reach + 1 - 2 * JITTER) * spacing < CUTOFF:
        reach += 1
    return lat, spacing, reach


def pair_fields(pj, pi):
    dx = pj[0:1, :] - pi[:, 0:1]
    dy = pj[1:2, :] - pi[:, 1:2]
    dz = pj[2:3, :] - pi[:, 2:3]
    sq = dx * dx + dy * dy + dz * dz
    near = jnp.logical_and(sq < CUTOFF * CUTOFF, sq > 0.01)
    weight = jnp.where(near, pj[3:4, :] * pi[:, 3:4], 0.0)
    safe = jnp.where(near, sq, 1.0)
    inv = lax.rsqrt(safe)
    r = safe * inv
    u = r * (1.0 / CUTOFF)
    u2 = u * u
    u5 = u2 * u2 * u
    env = 1.0 + u5 * u * (-28.0 + u * (48.0 - 21.0 * u))
    denv = u5 * (-168.0 + u * (336.0 - 168.0 * u)) * (1.0 / CUTOFF)
    amp = weight * inv * math.sqrt(2.0 / CUTOFF)
    q = amp * env
    p = amp * denv - q * inv
    t = u * math.pi - 0.5 * math.pi
    t2 = t * t
    cos_t = 1.0 + t2 * (
        -1.0 / 2 + t2 * (1.0 / 24 + t2 * (-1.0 / 720 + t2 * (1.0 / 40320 + t2 * (-1.0 / 3628800 + t2 * (1.0 / 479001600)))))
    )
    sin_t = t * (
        1.0 + t2 * (-1.0 / 6 + t2 * (1.0 / 120 + t2 * (-1.0 / 5040 + t2 * (1.0 / 362880 + t2 * (-1.0 / 39916800)))))
    )
    return dx * inv, dy * inv, dz * inv, inv, q, p, cos_t, -sin_t


def compute_kernel(
    dims,
    layer_ref,
    tile_ref,
    small_ref,
    pick_hbm,
    pick_t_hbm,
    spot_hbm,
    shift_hbm,
    turn_hbm,
    origin_hbm,
    radial_hbm,
    coupling_hbm,
    mixing_hbm,
    hw_hbm,
    ow_hbm,
    gsend_ref,
    gown_ref,
    force_ref,
    out_ref,
    pick_ref,
    pick_t_ref,
    spot_ref,
    shift_ref,
    turn_ref,
    origin_ref,
    radial_ref,
    coupling_ref,
    mixing_ref,
    hw_ref,
    ow_ref,
    rpos_ref,
    wsum_ref,
    node_ref,
    posj_ref,
    fj_ref,
    slab_ref,
    even_ref,
    odd_ref,
    field_ref,
    sv_ref,
    en_ref,
    acc_ref,
    geven_ref,
    godd_ref,
    load_sem,
):
    sx, sy, sz, reach, nb, lat = dims
    nbx, nby = sx // BLOCK, sy // BLOCK
    wide = BLOCK + 2 * reach
    depth = sz + 2 * reach
    rows = wide * depth
    near = wide * rows
    own = BLOCK * BLOCK * sz
    px = sx + 2 * reach
    cx = sx // lat
    o = sy * sz
    chunks = [(c, min(128, near - c)) for c in range(0, near, 128)]
    root3 = math.sqrt(3.0)

    loads = [
        pltpu.make_async_copy(source, target, load_sem.at[n])
        for n, (source, target) in enumerate(
            [
                (pick_hbm, pick_ref),
                (spot_hbm, spot_ref),
                (shift_hbm, shift_ref),
                (turn_hbm, turn_ref),
                (origin_hbm, origin_ref),
                (radial_hbm, radial_ref),
                (coupling_hbm, coupling_ref),
                (mixing_hbm, mixing_ref),
                (hw_hbm, hw_ref),
                (ow_hbm, ow_ref),
                (pick_t_hbm, pick_t_ref),
            ]
        )
    ]
    for load in loads:
        load.start()
    wsum_ref[...] = jnp.zeros(wsum_ref.shape, jnp.float32)
    fj_ref[...] = jnp.zeros(fj_ref.shape, jnp.float32)
    force_ref[...] = jnp.zeros(force_ref.shape, jnp.float32)
    for load in loads:
        load.wait()

    for x in range(px):
        full = jnp.dot(pick_ref[...], layer_ref[x], preferred_element_type=jnp.float32)
        full = full.astype(jnp.bfloat16)
        for by in range(nby):
            slab_ref[by, x] = full[by * rows : (by + 1) * rows]
            acc_ref[by, x] = jnp.zeros((rows, full.shape[1]), jnp.float32)

    def layer_spot(x):
        at = x - reach
        side = 1 if at < 0 else 2 if at >= sx else 0
        at = at % sx
        return side, at // lat, slice((at % lat) * o, (at % lat + 1) * o)

    spot = spot_ref[...].astype(jnp.float32)
    lines = []
    for x in range(px):
        side, cell, lanes = layer_spot(x)
        lines.append(
            jnp.concatenate(
                [tile_ref[side, n // 3, n % 3, cell][:, lanes] for n in range(9)], axis=1
            )
        )
    columns = (
        jnp.dot(
            jnp.concatenate(lines, axis=0), spot, precision=HIGH, preferred_element_type=jnp.float32
        )
        + shift_ref[...]
    )
    for by in range(nby):
        for bx in range(nbx):
            for k in range(wide):
                x = bx * BLOCK + k
                posj_ref[by * nbx + bx, :, k * rows : (k + 1) * rows] = columns[
                    x * 4 : x * 4 + 4, by * rows : (by + 1) * rows
                ]
    turn = turn_ref[...].astype(jnp.float32)
    mine = jnp.concatenate([small_ref[n].T for n in range(cx)], axis=0)
    mine = jnp.dot(turn, mine, precision=HIGH, preferred_element_type=jnp.float32) + origin_ref[...]
    rpos_ref[...] = mine.reshape(nbx * nby, own, mine.shape[1])

    blocks = nbx * nby
    half = blocks // 2

    def basis(blk, edge_ref, slot):
        pi = rpos_ref[blk]
        for c, w in chunks:
            pj = posj_ref[blk, :, c : c + w]
            nx, ny, nz, inv, q, p, s1, c1 = pair_fields(pj, pi)
            field_ref[blk, 0, :, c : c + w] = nx
            field_ref[blk, 1, :, c : c + w] = ny
            field_ref[blk, 2, :, c : c + w] = nz
            field_ref[blk, 3, :, c : c + w] = inv
            field_ref[blk, 4, :, c : c + w] = q
            field_ref[blk, 5, :, c : c + w] = p
            field_ref[blk, 6, :, c : c + w] = s1
            field_ref[blk, 7, :, c : c + w] = c1
            twice = 2.0 * c1
            before, now = jnp.zeros_like(s1), s1
            q3 = root3 * q
            qs = (q, q3 * nx, q3 * ny, q3 * nz)
            for b in range(nb):
                for m in range(4):
                    k = (b * 4 + m) * own
                    edge_ref[slot, k : k + own, c : c + w] = (qs[m] * now).astype(jnp.bfloat16)
                before, now = now, twice * now - before

    def gather(blk, edge_ref, slot):
        by, bx = blk // nbx, lax.rem(blk, nbx)
        slab = slab_ref[by, pl.ds(bx * BLOCK, wide)].reshape(near, -1)
        summed = jnp.dot(edge_ref[slot], slab, preferred_element_type=jnp.float32)
        for m in range(4):
            total = None
            for b in range(nb):
                k = (b * 4 + m) * own
                term = summed[k : k + own] * radial_ref[min(m, 1), b : b + 1, :]
                total = term if total is None else total + term
            sv_ref[m, pl.ds(blk * own, own)] = total

    def forward(i, carry):
        gather(2 * i, even_ref, i)
        basis(2 * i + 1, odd_ref, i)
        gather(2 * i + 1, odd_ref, i)
        basis(2 * i + 2, even_ref, i + 1)
        return carry

    basis(0, even_ref, 0)
    lax.fori_loop(0, half - 1, forward, 0)
    gather(blocks - 2, even_ref, half - 1)
    basis(blocks - 1, odd_ref, half - 1)
    gather(blocks - 1, odd_ref, half - 1)

    flat = rpos_ref[...].reshape(nbx * nby * own, -1)
    occ = flat[:, 3:4]
    kind = flat[:, 4:5]
    spec = lax.broadcasted_iota(jnp.int32, (flat.shape[0], coupling_ref.shape[0]), 1)
    onehot = (kind.astype(jnp.int32) == spec).astype(jnp.float32)
    wq = [
        jnp.dot(onehot, coupling_ref[:, n], precision=HIGH, preferred_element_type=jnp.float32)
        for n in range(3)
    ]
    scalar = sv_ref[0]
    length_sq = sv_ref[1] * sv_ref[1] + sv_ref[2] * sv_ref[2] + sv_ref[3] * sv_ref[3]
    product = wq[0] * scalar + wq[1] * scalar * scalar + wq[2] * length_sq
    fold = lax.dot_general(
        mixing_ref[...],
        hw_ref[...],
        (((1,), (1,)), ((), ())),
        precision=HIGH,
        preferred_element_type=jnp.float32,
    )
    hidden = jnp.dot(product, fold, precision=HIGH, preferred_element_type=jnp.float32)
    logistic = jax.nn.sigmoid(hidden)
    energy = occ * jnp.sum(ow_ref[...] * hidden * logistic, axis=1, keepdims=True)
    d_hidden = occ * ow_ref[...] * logistic * (1.0 + hidden * (1.0 - logistic))
    d_product = lax.dot_general(
        d_hidden, fold, (((1,), (1,)), ((), ())), precision=HIGH, preferred_element_type=jnp.float32
    )
    en_ref[...] = jnp.broadcast_to(energy, en_ref.shape)
    sv_ref[0] = d_product * (wq[0] + 2.0 * wq[1] * scalar)
    twice_d = 2.0 * wq[2] * d_product
    for m in range(1, 4):
        sv_ref[m] = twice_d * sv_ref[m]

    def scatter(blk, edge_ref, slot, g_ref):
        by, bx = blk // nbx, lax.rem(blk, nbx)
        parts = []
        for b in range(nb):
            for m in range(4):
                parts.append(
                    sv_ref[m, pl.ds(blk * own, own)] * radial_ref[min(m, 1), b : b + 1, :]
                )
        d_full = jnp.concatenate(parts, axis=0)
        d_half = d_full.astype(jnp.bfloat16)
        slab = slab_ref[by, pl.ds(bx * BLOCK, wide)].reshape(near, -1)
        g_ref[...] = lax.dot_general(
            d_half, slab, (((1,), (1,)), ((), ())), preferred_element_type=jnp.float32
        )
        d_turn = d_full.T.astype(jnp.bfloat16)
        turned = jnp.dot(d_turn, edge_ref[slot], preferred_element_type=jnp.float32)
        acc_ref[by, pl.ds(bx * BLOCK, wide)] += turned.T.reshape(wide, rows, -1)

    def forces(blk, g_ref):
        by, bx = blk // nbx, lax.rem(blk, nbx)
        total = [jnp.zeros((own, 1), jnp.float32) for _ in range(3)]
        for c, w in chunks:
            nx, ny, nz, inv, q, p, s1, c1 = (field_ref[blk, n, :, c : c + w] for n in range(8))
            twice = 2.0 * c1
            s_before, s_now = jnp.zeros_like(s1), s1
            c_before, c_now = jnp.ones_like(c1), c1
            s_sum = [None] * 4
            c_sum = [None] * 4
            for b in range(nb):
                scaled = (b + 1.0) * c_now
                for m in range(4):
                    k = (b * 4 + m) * own
                    g = g_ref[k : k + own, c : c + w]
                    s_sum[m] = g * s_now if b == 0 else s_sum[m] + g * s_now
                    c_sum[m] = g * scaled if b == 0 else c_sum[m] + g * scaled
                s_before, s_now = s_now, twice * s_now - s_before
                c_before, c_now = c_now, twice * c_now - c_before
            s_dot = nx * s_sum[1] + ny * s_sum[2] + nz * s_sum[3]
            c_dot = nx * c_sum[1] + ny * c_sum[2] + nz * c_sum[3]
            slope = (q * (math.pi / CUTOFF)) * (c_sum[0] + root3 * c_dot) + p * (
                s_sum[0] + root3 * s_dot
            )
            across = root3 * q * inv
            along = slope - across * s_dot
            outs = [
                along * n + across * s_sum[m + 1] for m, n in enumerate((nx, ny, nz))
            ]
            for m in range(3):
                fj_ref[m : m + 1, c : c + w] = -jnp.sum(outs[m], axis=0, keepdims=True)
                total[m] = total[m] + jnp.sum(outs[m], axis=1, keepdims=True)
        for k in range(wide):
            wsum_ref[by, bx * BLOCK + k] += fj_ref[:, k * rows : (k + 1) * rows]
        lane = lax.broadcasted_iota(jnp.int32, (own, node_ref.shape[1]), 1)
        here = pl.ds(blk * own, own)
        node_ref[here] = jnp.where(
            lane == 0,
            total[0],
            jnp.where(lane == 1, total[1], jnp.where(lane == 2, total[2], en_ref[here])),
        )

    def backward(i, carry):
        scatter(2 * i + 1, odd_ref, i, godd_ref)
        forces(2 * i, geven_ref)
        scatter(2 * i + 2, even_ref, i + 1, geven_ref)
        forces(2 * i + 1, godd_ref)
        return carry

    scatter(0, even_ref, 0, geven_ref)
    lax.fori_loop(0, half - 1, backward, 0)
    scatter(blocks - 1, odd_ref, half - 1, godd_ref)
    forces(blocks - 2, geven_ref)
    forces(blocks - 1, godd_ref)

    for x in range(px):
        stack = jnp.concatenate([acc_ref[by, x] for by in range(nby)], axis=0)
        top = stack.astype(jnp.bfloat16)
        rest = (stack - top.astype(jnp.float32)).astype(jnp.bfloat16)
        total = jnp.dot(pick_t_ref[...], top, preferred_element_type=jnp.float32) + jnp.dot(
            pick_t_ref[...], rest, preferred_element_type=jnp.float32
        )
        gsend_ref[x] = total.astype(jnp.bfloat16)
        if reach <= x < reach + sx:
            gown_ref[x - reach] = total[0:o]

    lines = jnp.concatenate(
        [jnp.concatenate([wsum_ref[by, x] for by in range(nby)], axis=1) for x in range(px)], axis=0
    )
    lines = lax.dot_general(
        lines, spot, (((1,), (1,)), ((), ())), precision=HIGH, preferred_element_type=jnp.float32
    )
    for x in range(px):
        side, cell, lanes = layer_spot(x)
        for n in range(9):
            force_ref[side, n // 3, n % 3, cell, :, lanes] = lines[
                x * 4 : x * 4 + 4, n * o : (n + 1) * o
            ]
    nodes = lax.dot_general(
        node_ref[...], turn, (((0,), (0,)), ((), ())), precision=HIGH, preferred_element_type=jnp.float32
    )
    for n in range(cx):
        out_ref[n] = nodes[0:4, n * lat * o : (n + 1) * lat * o]


def ring(axis):
    count = lax.axis_size(axis)
    me = lax.axis_index(axis)
    return lax.rem(me + count - 1, count), lax.rem(me + 1, count)


DIRECTIONS = [
    (a, b, c)
    for a in (-1, 1, 0)
    for b in (0, -1, 1)
    for c in (0, -1, 1)
    if (a, b, c) != (0, 0, 0)
]


def slot_of(step):
    return {0: 0, -1: 1, 1: 2}[step]


def partners():
    around = {axis: (lax.axis_index(axis),) + ring(axis) for axis in ("gx", "gy", "gz")}
    return {
        d: {axis: around[axis][slot_of(step)] for axis, step in zip(("gx", "gy", "gz"), d)}
        for d in DIRECTIONS
    }


def greet(around):
    barrier = pltpu.get_barrier_semaphore()
    for target in around.values():
        pl.semaphore_signal(
            barrier, inc=1, device_id=target, device_id_type=pl.DeviceIdType.MESH
        )
    return barrier


def sender(send_sem, recv_sem):
    def send(slot, source, target, device):
        copy = pltpu.make_async_remote_copy(
            src_ref=source,
            dst_ref=target,
            send_sem=send_sem.at[slot],
            recv_sem=recv_sem.at[slot],
            device_id=device,
            device_id_type=pl.DeviceIdType.MESH,
        )
        copy.start()
        return copy

    return send


def spread_kernel(
    dims,
    spacing,
    counts_ref,
    pos_hbm,
    kind_hbm,
    feat_hbm,
    faces_hbm,
    layer_ref,
    tile_ref,
    place_ref,
    small_ref,
    pos_ref,
    kind_ref,
    feat_ref,
    faces_ref,
    out_ref,
    load_sem,
    send_sem,
    recv_sem,
):
    sx, lat, reach, o, pieces = dims
    around = partners()
    loads = [
        pltpu.make_async_copy(source, target, load_sem.at[n])
        for n, (source, target) in enumerate(
            [(pos_hbm, pos_ref), (kind_hbm, kind_ref), (feat_hbm, feat_ref), (faces_hbm, faces_ref)]
        )
    ]
    for load in loads:
        load.start()
    barrier = greet(around)
    send = sender(send_sem, recv_sem)
    for load in loads:
        load.wait()
    cx, cy, _, cz, capacity = pos_ref.shape
    sy, sz = cy * lat, cz * lat
    slot = lax.broadcasted_iota(jnp.int32, (1, capacity), 1)
    for col in range(cx):
        parts, codes = [], []
        for cell_y in range(cy):
            for cell_z in range(cz):
                xyz = [pos_ref[col, cell_y, n, cell_z : cell_z + 1] for n in range(3)]
                site = [
                    jnp.clip(jnp.floor(v * (1.0 / spacing)), 0.0, lat - 1.0) for v in xyz
                ]
                codes.append((site[0] * sy + site[1] + cell_y * lat) * sz + site[2] + cell_z * lat)
                occ = (slot < counts_ref[col, cell_z, cell_y]).astype(jnp.float32)
                kind = kind_ref[col, cell_y, cell_z : cell_z + 1].astype(jnp.float32)
                parts.append(
                    jnp.concatenate(xyz + [occ, kind, jnp.zeros((3, capacity), jnp.float32)], axis=0)
                )
        code = jnp.concatenate(codes, axis=1)
        small = jnp.concatenate(parts, axis=1)
        count = code.shape[1]
        place = (
            code == lax.broadcasted_iota(jnp.int32, (count, count), 0).astype(jnp.float32)
        ).astype(jnp.float32)
        small = lax.dot_general(
            small, place, (((1,), (1,)), ((), ())), precision=HIGH, preferred_element_type=jnp.float32
        )
        small_ref[col] = small
        tile_ref[0, 0, 0, col] = small[0:4]
        place_ref[col] = place.astype(jnp.bfloat16)
        sites = jnp.dot(place_ref[col], feat_ref[col], preferred_element_type=jnp.float32)
        sites = sites.astype(jnp.bfloat16)
        for k in range(lat):
            x = col * lat + k
            mine = sites[k * o : (k + 1) * o]
            layer_ref[reach + x, 0:o] = mine
            out_ref[x, 0:o] = mine
            faces = jnp.dot(faces_ref[...], mine, preferred_element_type=jnp.float32)
            out_ref[x, o:] = faces.astype(jnp.bfloat16)
    pl.semaphore_wait(barrier, len(around))

    from_x = {-1: pl.ds(0, reach), 1: pl.ds(sx - reach, reach), 0: pl.ds(0, sx)}
    to_x = {-1: pl.ds(reach + sx, reach), 1: pl.ds(0, reach), 0: pl.ds(reach, sx)}
    cell = {-1: pl.ds(0, 1), 1: pl.ds(cx - 1, 1), 0: pl.ds(0, cx)}
    copies = []
    for n, (a, b, c) in enumerate(DIRECTIONS):
        start, size = pieces[(b, c)]
        copies.append(
            send(
                2 * n,
                out_ref.at[from_x[a], pl.ds(start, size)],
                layer_ref.at[to_x[a], pl.ds(pieces[(-b, -c)][0], size)],
                around[(a, b, c)],
            )
        )
        copies.append(
            send(
                2 * n + 1,
                tile_ref.at[0, 0, 0, cell[a]],
                tile_ref.at[slot_of(-a), slot_of(-b), slot_of(-c), cell[a]],
                around[(a, b, c)],
            )
        )
    for copy in copies:
        copy.wait_recv()
    for copy in copies:
        copy.wait_send()


def gather_kernel(
    dims,
    place_ref,
    gsend_ref,
    gown_ref,
    force_ref,
    node_ref,
    faces_ref,
    out_ref,
    energy_ref,
    xyz_ref,
    inner_ref,
    outer_ref,
    back_ref,
    send_sem,
    recv_sem,
):
    sx, lat, reach, o, pieces = dims
    cx = sx // lat
    around = partners()
    back_ref[...] = jnp.zeros(back_ref.shape, jnp.float32)
    barrier = greet(around)
    send = sender(send_sem, recv_sem)
    pl.semaphore_wait(barrier, len(around))

    from_x = {-1: pl.ds(0, reach), 1: pl.ds(reach + sx, reach), 0: pl.ds(reach, sx)}
    cell = {-1: pl.ds(cx - 1, 1), 1: pl.ds(0, 1), 0: pl.ds(0, cx)}
    copies = []
    for n, (a, b, c) in enumerate(DIRECTIONS):
        start, size = pieces[(b, c)]
        rows = pl.ds(pieces[(-b, -c)][0], size)
        into = inner_ref.at[:, rows] if a == 0 else outer_ref.at[slot_of(-a) - 1, :, rows]
        copies.append(
            send(2 * n, gsend_ref.at[from_x[a], pl.ds(start, size)], into, around[(a, b, c)])
        )
        copies.append(
            send(
                2 * n + 1,
                force_ref.at[slot_of(a), slot_of(b), slot_of(c), cell[a]],
                back_ref.at[slot_of(-a), slot_of(-b), slot_of(-c), cell[a]],
                around[(a, b, c)],
            )
        )
    for copy in copies:
        copy.wait_recv()

    tile = node_ref[...] + force_ref[0, 0, 0]
    for a, b, c in DIRECTIONS:
        tile = tile + back_ref[slot_of(a), slot_of(b), slot_of(c)]

    def spread(received):
        return lax.dot_general(
            faces_ref[...], received, (((0,), (0,)), ((), ())), preferred_element_type=jnp.float32
        )

    _, cy, _, cz, capacity = xyz_ref.shape
    for col in range(cx):
        sites = []
        for k in range(lat):
            x = col * lat + k
            total = gown_ref[x] + spread(inner_ref[x, o:])
            for side, at in ((0, x), (1, x - (sx - reach))):
                if 0 <= at < reach:
                    total = total + outer_ref[side, at, 0:o].astype(jnp.float32)
                    total = total + spread(outer_ref[side, at, o:])
            sites.append(total)
        whole = jnp.concatenate(sites, axis=0)
        top = whole.astype(jnp.bfloat16)
        rest = (whole - top.astype(jnp.float32)).astype(jnp.bfloat16)
        place = place_ref[col].astype(jnp.float32)
        turn = place.T.astype(jnp.bfloat16)
        out_ref[col] = jnp.dot(turn, top, preferred_element_type=jnp.float32) + jnp.dot(
            turn, rest, preferred_element_type=jnp.float32
        )
        slots = jnp.dot(tile[col], place, precision=HIGH, preferred_element_type=jnp.float32)
        for n in range(cy * cz):
            lanes = slice(n * capacity, (n + 1) * capacity)
            for m in range(3):
                xyz_ref[col, n // cz, m, n % cz : n % cz + 1] = slots[m : m + 1, lanes]
            energy_ref[col, n // cz, n % cz : n % cz + 1] = slots[3:4, lanes]
    for copy in copies:
        copy.wait_send()


def tables(sx, sy, sz, reach, lat):
    px, py, depth = sx + 2 * reach, sy + 2 * reach, sz + 2 * reach
    wide, nbx, nby = BLOCK + 2 * reach, sx // BLOCK, sy // BLOCK
    o = sy * sz
    extent = {0: (sy, sz), -1: (reach, reach), 1: (reach, reach)}
    pieces, total = {}, 0
    for b in (0, -1, 1):
        for c in (0, -1, 1):
            size = extent[b][0] * extent[c][1]
            pieces[(b, c)] = (total, -(-size // 16) * 16)
            total += pieces[(b, c)][1]

    def spot(n, size):
        if n < reach:
            return -1, n
        if n >= reach + size:
            return 1, n - reach - size
        return 0, n - reach

    pick = np.zeros((nby, wide, depth, total), np.float32)
    pick_pos = np.zeros((9 * o, nby, wide, depth), np.float32)
    for by in range(nby):
        for y in range(wide):
            for z in range(depth):
                b, at_y = spot(by * BLOCK + y, sy)
                c, at_z = spot(z, sz)
                pick[by, y, z, pieces[(b, c)][0] + at_y * extent[c][1] + at_z] = 1
                tile_y = sy - reach + at_y if b < 0 else at_y
                tile_z = sz - reach + at_z if c < 0 else at_z
                line = (slot_of(b) * 3 + slot_of(c)) * o + tile_y * sz + tile_z
                pick_pos[line, by, y, z] = 1
    faces = np.zeros((total - o, o), np.float32)
    for (b, c), (start, _) in pieces.items():
        if (b, c) == (0, 0):
            continue
        for y in range(extent[b][0]):
            for z in range(extent[c][1]):
                from_y = sy - reach + y if b > 0 else y
                from_z = sz - reach + z if c > 0 else z
                faces[start - o + y * extent[c][1] + z, from_y * sz + from_z] = 1
    steps = [np.floor((np.arange(n) - reach) / lat).astype(np.float32) * SIDE for n in (px, py, depth)]
    shifts = np.zeros((px, 4, py, depth), np.float32)
    shifts[:, 0] = steps[0][:, None, None]
    shifts[:, 1] = steps[1][None, :, None]
    shifts[:, 2] = steps[2][None, None, :]
    shift = np.stack([shifts[:, :, by * BLOCK : by * BLOCK + wide] for by in range(nby)], axis=2)
    count = sx * sy * sz
    index = np.arange(count).reshape(nbx, BLOCK, nby, BLOCK, sz).transpose(2, 0, 1, 3, 4).reshape(-1)
    turn = np.zeros((count, count), np.float32)
    turn[np.arange(count), index] = 1
    inner = shifts[reach : reach + sx, :, reach : reach + sy, reach : reach + sz]
    origin = np.zeros((count, 8), np.float32)
    origin[:, :4] = inner.transpose(0, 2, 3, 1).reshape(count, 4)[index]
    return (
        pieces,
        total,
        pick.reshape(-1, total),
        pick_pos.reshape(9 * o, -1),
        faces,
        shift.reshape(px * 4, -1),
        turn,
        origin,
    )


def body(
    local_pos,
    counts,
    species,
    features,
    radial_weights,
    coupling,
    mixing,
    hidden_weights,
    output_weights,
):
    cx, cy, cz = counts.shape
    capacity, channels = features.shape[3:]
    nb = radial_weights.shape[1]
    lat, spacing, reach = lattice_of(capacity)
    sx, sy, sz = cx * lat, cy * lat, cz * lat
    nbx, nby = sx // BLOCK, sy // BLOCK
    wide, depth = BLOCK + 2 * reach, sz + 2 * reach
    near, own = wide * wide * depth, BLOCK * BLOCK * sz
    px = sx + 2 * reach
    rows = wide * depth
    blocks = nbx * nby
    o = sy * sz
    pieces, total, pick, pick_pos, faces, shift, turn, origin = tables(sx, sy, sz, reach, lat)
    column = cy * cz * capacity
    total_own = sx * sy * sz
    f32, half = jnp.float32, jnp.bfloat16

    vmem = pl.BlockSpec(memory_space=pltpu.VMEM)
    hbm = pl.BlockSpec(memory_space=pl.ANY)
    dims = (sx, lat, reach, o, pieces)
    limit = 50 * 1024 * 1024
    ways = 2 * len(DIRECTIONS)
    faces = jnp.asarray(faces, half)
    local_turned = local_pos.transpose(0, 1, 3, 2, 4)
    feat_flat = features.reshape(cx, column, channels)
    tile_shape = (3, 3, 3, cx, 4, lat * o)
    layers, tiles, place, small_sites = pl.pallas_call(
        functools.partial(spread_kernel, dims, spacing),
        out_shape=(
            jax.ShapeDtypeStruct((px, total, channels), half),
            jax.ShapeDtypeStruct(tile_shape, f32),
            jax.ShapeDtypeStruct((cx, column, column), half),
            jax.ShapeDtypeStruct((cx, 8, column), f32),
        ),
        in_specs=[pl.BlockSpec(memory_space=pltpu.SMEM)] + [hbm] * 4,
        out_specs=(vmem,) * 4,
        scratch_shapes=[
            pltpu.VMEM(local_turned.shape, f32),
            pltpu.VMEM(species.shape, jnp.int32),
            pltpu.VMEM(feat_flat.shape, half),
            pltpu.VMEM(faces.shape, half),
            pltpu.VMEM((sx, total, channels), half),
            pltpu.SemaphoreType.DMA((4,)),
            pltpu.SemaphoreType.DMA((ways,)),
            pltpu.SemaphoreType.DMA((ways,)),
        ],
        compiler_params=pltpu.CompilerParams(
            collective_id=0, has_side_effects=True, vmem_limit_bytes=limit
        ),
        name="halo_out",
    )(counts.transpose(0, 2, 1), local_turned, species, feat_flat, faces)

    fixed = [
        jnp.asarray(pick, half),
        jnp.asarray(pick.T, half),
        jnp.asarray(pick_pos, half),
        jnp.asarray(shift),
        jnp.asarray(turn, half),
        jnp.asarray(origin),
        radial_weights,
        coupling.transpose(1, 0, 2),
        mixing,
        hidden_weights.T,
        output_weights[None, :],
    ]
    gsend, gown, force, node = pl.pallas_call(
        functools.partial(compute_kernel, (sx, sy, sz, reach, nb, lat)),
        out_shape=(
            jax.ShapeDtypeStruct((px, total, channels), half),
            jax.ShapeDtypeStruct((sx, o, channels), f32),
            jax.ShapeDtypeStruct(tile_shape, f32),
            jax.ShapeDtypeStruct((cx, 4, lat * o), f32),
        ),
        in_specs=[vmem] * 3 + [hbm] * len(fixed),
        out_specs=(vmem,) * 4,
        scratch_shapes=[pltpu.VMEM(item.shape, item.dtype) for item in fixed]
        + [
            pltpu.VMEM((blocks, own, 8), f32),
            pltpu.VMEM((nby, px, 4, rows), f32),
            pltpu.VMEM((total_own, 128), f32),
            pltpu.VMEM((blocks, 4, near), f32),
            pltpu.VMEM((4, near), f32),
            pltpu.VMEM((nby, px, rows, channels), half),
            pltpu.VMEM((blocks // 2, nb * 4 * own, near), half),
            pltpu.VMEM((blocks // 2, nb * 4 * own, near), half),
            pltpu.VMEM((blocks, 8, own, near), f32),
            pltpu.VMEM((4, total_own, channels), f32),
            pltpu.VMEM((total_own, 128), f32),
            pltpu.VMEM((nby, px, rows, channels), f32),
            pltpu.VMEM((nb * 4 * own, near), f32),
            pltpu.VMEM((nb * 4 * own, near), f32),
            pltpu.SemaphoreType.DMA((len(fixed),)),
        ],
        compiler_params=pltpu.CompilerParams(vmem_limit_bytes=limit),
        name="pair_layer",
    )(layers, tiles, small_sites, *fixed)

    grad, energy, forces = pl.pallas_call(
        functools.partial(gather_kernel, dims),
        out_shape=(
            jax.ShapeDtypeStruct((cx, column, channels), f32),
            jax.ShapeDtypeStruct((cx, cy, cz, capacity), f32),
            jax.ShapeDtypeStruct((cx, cy, 3, cz, capacity), f32),
        ),
        in_specs=[vmem] * 6,
        out_specs=(vmem, vmem, vmem),
        scratch_shapes=[
            pltpu.VMEM((sx, total, channels), half),
            pltpu.VMEM((2, reach, total, channels), half),
            pltpu.VMEM(tile_shape, f32),
            pltpu.SemaphoreType.DMA((ways,)),
            pltpu.SemaphoreType.DMA((ways,)),
        ],
        compiler_params=pltpu.CompilerParams(
            collective_id=1, has_side_effects=True, vmem_limit_bytes=limit
        ),
        name="halo_back",
    )(place, gsend, gown, force, node, faces)
    return (
        energy,
        forces.transpose(0, 1, 3, 2, 4),
        grad.reshape(cx, cy, cz, capacity, channels),
    )


def solution(mesh):
    placed = (
        P("gx", "gy", "gz", None, None),
        P("gx", "gy", "gz"),
        P("gx", "gy", "gz", None),
        P("gx", "gy", "gz", None, None),
        P(),
        P(),
        P(),
        P(),
        P(),
    )
    return jax.shard_map(
        body,
        mesh=mesh,
        in_specs=placed,
        out_specs=(
            P("gx", "gy", "gz", None),
            P("gx", "gy", "gz", None, None),
            P("gx", "gy", "gz", None, None),
        ),
        check_vma=False,
    )
```

```python
import functools
import math

import jax
import jax.numpy as jnp
import numpy as np
from jax import lax
from jax.experimental import pallas as pl
from jax.experimental.pallas import tpu as pltpu
from jax.sharding import PartitionSpec as P

SIDE = 7.0
CUTOFF = 5.0
JITTER = 0.3
BLOCK = 2
HIGH = lax.Precision.HIGHEST


def lattice_of(capacity):
    lat = round(capacity ** (1.0 / 3.0))
    spacing = SIDE / lat
    reach = 0
    while (reach + 1 - 2 * JITTER) * spacing < CUTOFF:
        reach += 1
    return lat, spacing, reach


def pair_fields(pj, pi):
    dx = pj[0:1, :] - pi[:, 0:1]
    dy = pj[1:2, :] - pi[:, 1:2]
    dz = pj[2:3, :] - pi[:, 2:3]
    sq = dx * dx + dy * dy + dz * dz
    near = jnp.logical_and(sq < CUTOFF * CUTOFF, sq > 0.01)
    weight = jnp.where(near, pj[3:4, :] * pi[:, 3:4], 0.0)
    safe = jnp.where(near, sq, 1.0)
    inv = lax.rsqrt(safe)
    r = safe * inv
    u = r * (1.0 / CUTOFF)
    u2 = u * u
    u5 = u2 * u2 * u
    env = 1.0 + u5 * u * (-28.0 + u * (48.0 - 21.0 * u))
    denv = u5 * (-168.0 + u * (336.0 - 168.0 * u)) * (1.0 / CUTOFF)
    amp = weight * inv * math.sqrt(2.0 / CUTOFF)
    q = amp * env
    p = amp * denv - q * inv
    t = u * math.pi - 0.5 * math.pi
    t2 = t * t
    cos_t = 1.0 + t2 * (
        -1.0 / 2 + t2 * (1.0 / 24 + t2 * (-1.0 / 720 + t2 * (1.0 / 40320 + t2 * (-1.0 / 3628800 + t2 * (1.0 / 479001600)))))
    )
    sin_t = t * (
        1.0 + t2 * (-1.0 / 6 + t2 * (1.0 / 120 + t2 * (-1.0 / 5040 + t2 * (1.0 / 362880 + t2 * (-1.0 / 39916800)))))
    )
    return dx * inv, dy * inv, dz * inv, inv, q, p, cos_t, -sin_t


def compute_kernel(
    dims,
    layer_ref,
    tile_ref,
    small_ref,
    pick_hbm,
    pick_t_hbm,
    spot_hbm,
    shift_hbm,
    turn_hbm,
    origin_hbm,
    radial_hbm,
    coupling_hbm,
    mixing_hbm,
    hw_hbm,
    ow_hbm,
    gsend_ref,
    gown_ref,
    force_ref,
    out_ref,
    pick_ref,
    pick_t_ref,
    spot_ref,
    shift_ref,
    turn_ref,
    origin_ref,
    radial_ref,
    coupling_ref,
    mixing_ref,
    hw_ref,
    ow_ref,
    rpos_ref,
    wsum_ref,
    node_ref,
    posj_ref,
    fj_ref,
    slab_ref,
    even_ref,
    odd_ref,
    field_ref,
    sv_ref,
    en_ref,
    acc_ref,
    geven_ref,
    godd_ref,
    load_sem,
):
    sx, sy, sz, reach, nb, lat = dims
    nbx, nby = sx // BLOCK, sy // BLOCK
    wide = BLOCK + 2 * reach
    depth = sz + 2 * reach
    rows = wide * depth
    near = wide * rows
    own = BLOCK * BLOCK * sz
    px = sx + 2 * reach
    cx = sx // lat
    o = sy * sz
    chunks = [(c, min(128, near - c)) for c in range(0, near, 128)]
    root3 = math.sqrt(3.0)

    loads = [
        pltpu.make_async_copy(source, target, load_sem.at[n])
        for n, (source, target) in enumerate(
            [
                (pick_hbm, pick_ref),
                (spot_hbm, spot_ref),
                (shift_hbm, shift_ref),
                (turn_hbm, turn_ref),
                (origin_hbm, origin_ref),
                (radial_hbm, radial_ref),
                (coupling_hbm, coupling_ref),
                (mixing_hbm, mixing_ref),
                (hw_hbm, hw_ref),
                (ow_hbm, ow_ref),
                (pick_t_hbm, pick_t_ref),
            ]
        )
    ]
    for load in loads:
        load.start()
    wsum_ref[...] = jnp.zeros(wsum_ref.shape, jnp.float32)
    fj_ref[...] = jnp.zeros(fj_ref.shape, jnp.float32)
    force_ref[...] = jnp.zeros(force_ref.shape, jnp.float32)
    for load in loads:
        load.wait()

    for x in range(px):
        full = jnp.dot(pick_ref[...], layer_ref[x], preferred_element_type=jnp.float32)
        full = full.astype(jnp.bfloat16)
        for by in range(nby):
            slab_ref[by, x] = full[by * rows : (by + 1) * rows]
            acc_ref[by, x] = jnp.zeros((rows, full.shape[1]), jnp.float32)

    def layer_spot(x):
        at = x - reach
        side = 1 if at < 0 else 2 if at >= sx else 0
        at = at % sx
        return side, at // lat, slice((at % lat) * o, (at % lat + 1) * o)

    spot = spot_ref[...].astype(jnp.float32)
    lines = []
    for x in range(px):
        side, cell, lanes = layer_spot(x)
        lines.append(
            jnp.concatenate(
                [tile_ref[side, n // 3, n % 3, cell][:, lanes] for n in range(9)], axis=1
            )
        )
    columns = (
        jnp.dot(
            jnp.concatenate(lines, axis=0), spot, precision=HIGH, preferred_element_type=jnp.float32
        )
        + shift_ref[...]
    )
    for by in range(nby):
        for bx in range(nbx):
            for k in range(wide):
                x = bx * BLOCK + k
                posj_ref[by * nbx + bx, :, k * rows : (k + 1) * rows] = columns[
                    x * 4 : x * 4 + 4, by * rows : (by + 1) * rows
                ]
    turn = turn_ref[...].astype(jnp.float32)
    mine = jnp.concatenate([small_ref[n].T for n in range(cx)], axis=0)
    mine = jnp.dot(turn, mine, precision=HIGH, preferred_element_type=jnp.float32) + origin_ref[...]
    rpos_ref[...] = mine.reshape(nbx * nby, own, mine.shape[1])

    blocks = nbx * nby
    half = blocks // 2

    def basis(blk, edge_ref, slot):
        pi = rpos_ref[blk]
        for c, w in chunks:
            pj = posj_ref[blk, :, c : c + w]
            nx, ny, nz, inv, q, p, s1, c1 = pair_fields(pj, pi)
            field_ref[blk, 0, :, c : c + w] = nx
            field_ref[blk, 1, :, c : c + w] = ny
            field_ref[blk, 2, :, c : c + w] = nz
            field_ref[blk, 3, :, c : c + w] = inv
            field_ref[blk, 4, :, c : c + w] = q
            field_ref[blk, 5, :, c : c + w] = p
            field_ref[blk, 6, :, c : c + w] = s1
            field_ref[blk, 7, :, c : c + w] = c1
            twice = 2.0 * c1
            before, now = jnp.zeros_like(s1), s1
            q3 = root3 * q
            qs = (q, q3 * nx, q3 * ny, q3 * nz)
            for b in range(nb):
                for m in range(4):
                    k = (b * 4 + m) * own
                    edge_ref[slot, k : k + own, c : c + w] = (qs[m] * now).astype(jnp.bfloat16)
                before, now = now, twice * now - before

    def gather(blk, edge_ref, slot):
        by, bx = blk // nbx, lax.rem(blk, nbx)
        slab = slab_ref[by, pl.ds(bx * BLOCK, wide)].reshape(near, -1)
        summed = jnp.dot(edge_ref[slot], slab, preferred_element_type=jnp.float32)
        for m in range(4):
            total = None
            for b in range(nb):
                k = (b * 4 + m) * own
                term = summed[k : k + own] * radial_ref[min(m, 1), b : b + 1, :]
                total = term if total is None else total + term
            sv_ref[m, pl.ds(blk * own, own)] = total

    def forward(i, carry):
        gather(2 * i, even_ref, i)
        basis(2 * i + 1, odd_ref, i)
        gather(2 * i + 1, odd_ref, i)
        basis(2 * i + 2, even_ref, i + 1)
        return carry

    basis(0, even_ref, 0)
    lax.fori_loop(0, half - 1, forward, 0)
    gather(blocks - 2, even_ref, half - 1)
    basis(blocks - 1, odd_ref, half - 1)
    gather(blocks - 1, odd_ref, half - 1)

    flat = rpos_ref[...].reshape(nbx * nby * own, -1)
    occ = flat[:, 3:4]
    kind = flat[:, 4:5]
    spec = lax.broadcasted_iota(jnp.int32, (flat.shape[0], coupling_ref.shape[0]), 1)
    onehot = (kind.astype(jnp.int32) == spec).astype(jnp.float32)
    wq = [
        jnp.dot(onehot, coupling_ref[:, n], precision=HIGH, preferred_element_type=jnp.float32)
        for n in range(3)
    ]
    scalar = sv_ref[0]
    length_sq = sv_ref[1] * sv_ref[1] + sv_ref[2] * sv_ref[2] + sv_ref[3] * sv_ref[3]
    product = wq[0] * scalar + wq[1] * scalar * scalar + wq[2] * length_sq
    fold = lax.dot_general(
        mixing_ref[...],
        hw_ref[...],
        (((1,), (1,)), ((), ())),
        precision=HIGH,
        preferred_element_type=jnp.float32,
    )
    hidden = jnp.dot(product, fold, precision=HIGH, preferred_element_type=jnp.float32)
    logistic = jax.nn.sigmoid(hidden)
    energy = occ * jnp.sum(ow_ref[...] * hidden * logistic, axis=1, keepdims=True)
    d_hidden = occ * ow_ref[...] * logistic * (1.0 + hidden * (1.0 - logistic))
    d_product = lax.dot_general(
        d_hidden, fold, (((1,), (1,)), ((), ())), precision=HIGH, preferred_element_type=jnp.float32
    )
    en_ref[...] = jnp.broadcast_to(energy, en_ref.shape)
    sv_ref[0] = d_product * (wq[0] + 2.0 * wq[1] * scalar)
    twice_d = 2.0 * wq[2] * d_product
    for m in range(1, 4):
        sv_ref[m] = twice_d * sv_ref[m]

    def scatter(blk, edge_ref, slot, g_ref):
        by, bx = blk // nbx, lax.rem(blk, nbx)
        parts = []
        for b in range(nb):
            for m in range(4):
                parts.append(
                    sv_ref[m, pl.ds(blk * own, own)] * radial_ref[min(m, 1), b : b + 1, :]
                )
        d_full = jnp.concatenate(parts, axis=0)
        d_half = d_full.astype(jnp.bfloat16)
        slab = slab_ref[by, pl.ds(bx * BLOCK, wide)].reshape(near, -1)
        g_ref[...] = lax.dot_general(
            d_half, slab, (((1,), (1,)), ((), ())), preferred_element_type=jnp.float32
        )
        d_turn = d_full.T.astype(jnp.bfloat16)
        turned = jnp.dot(d_turn, edge_ref[slot], preferred_element_type=jnp.float32)
        acc_ref[by, pl.ds(bx * BLOCK, wide)] += turned.T.reshape(wide, rows, -1)

    def forces(blk, g_ref):
        by, bx = blk // nbx, lax.rem(blk, nbx)
        total = [jnp.zeros((own, 1), jnp.float32) for _ in range(3)]
        for c, w in chunks:
            nx, ny, nz, inv, q, p, s1, c1 = (field_ref[blk, n, :, c : c + w] for n in range(8))
            twice = 2.0 * c1
            s_before, s_now = jnp.zeros_like(s1), s1
            c_before, c_now = jnp.ones_like(c1), c1
            s_sum = [None] * 4
            c_sum = [None] * 4
            for b in range(nb):
                scaled = (b + 1.0) * c_now
                for m in range(4):
                    k = (b * 4 + m) * own
                    g = g_ref[k : k + own, c : c + w]
                    s_sum[m] = g * s_now if b == 0 else s_sum[m] + g * s_now
                    c_sum[m] = g * scaled if b == 0 else c_sum[m] + g * scaled
                s_before, s_now = s_now, twice * s_now - s_before
                c_before, c_now = c_now, twice * c_now - c_before
            s_dot = nx * s_sum[1] + ny * s_sum[2] + nz * s_sum[3]
            c_dot = nx * c_sum[1] + ny * c_sum[2] + nz * c_sum[3]
            slope = (q * (math.pi / CUTOFF)) * (c_sum[0] + root3 * c_dot) + p * (
                s_sum[0] + root3 * s_dot
            )
            across = root3 * q * inv
            along = slope - across * s_dot
            outs = [
                along * n + across * s_sum[m + 1] for m, n in enumerate((nx, ny, nz))
            ]
            for m in range(3):
                fj_ref[m : m + 1, c : c + w] = -jnp.sum(outs[m], axis=0, keepdims=True)
                total[m] = total[m] + jnp.sum(outs[m], axis=1, keepdims=True)
        for k in range(wide):
            wsum_ref[by, bx * BLOCK + k] += fj_ref[:, k * rows : (k + 1) * rows]
        lane = lax.broadcasted_iota(jnp.int32, (own, node_ref.shape[1]), 1)
        here = pl.ds(blk * own, own)
        node_ref[here] = jnp.where(
            lane == 0,
            total[0],
            jnp.where(lane == 1, total[1], jnp.where(lane == 2, total[2], en_ref[here])),
        )

    def backward(i, carry):
        scatter(2 * i + 1, odd_ref, i, godd_ref)
        forces(2 * i, geven_ref)
        scatter(2 * i + 2, even_ref, i + 1, geven_ref)
        forces(2 * i + 1, godd_ref)
        return carry

    scatter(0, even_ref, 0, geven_ref)
    lax.fori_loop(0, half - 1, backward, 0)
    scatter(blocks - 1, odd_ref, half - 1, godd_ref)
    forces(blocks - 2, geven_ref)
    forces(blocks - 1, godd_ref)

    for x in range(px):
        stack = jnp.concatenate([acc_ref[by, x] for by in range(nby)], axis=0)
        top = stack.astype(jnp.bfloat16)
        rest = (stack - top.astype(jnp.float32)).astype(jnp.bfloat16)
        total = jnp.dot(pick_t_ref[...], top, preferred_element_type=jnp.float32) + jnp.dot(
            pick_t_ref[...], rest, preferred_element_type=jnp.float32
        )
        gsend_ref[x] = total.astype(jnp.bfloat16)
        if reach <= x < reach + sx:
            gown_ref[x - reach] = total[0:o]

    lines = jnp.concatenate(
        [jnp.concatenate([wsum_ref[by, x] for by in range(nby)], axis=1) for x in range(px)], axis=0
    )
    lines = lax.dot_general(
        lines, spot, (((1,), (1,)), ((), ())), precision=HIGH, preferred_element_type=jnp.float32
    )
    for x in range(px):
        side, cell, lanes = layer_spot(x)
        for n in range(9):
            force_ref[side, n // 3, n % 3, cell, :, lanes] = lines[
                x * 4 : x * 4 + 4, n * o : (n + 1) * o
            ]
    nodes = lax.dot_general(
        node_ref[...], turn, (((0,), (0,)), ((), ())), precision=HIGH, preferred_element_type=jnp.float32
    )
    for n in range(cx):
        out_ref[n] = nodes[0:4, n * lat * o : (n + 1) * lat * o]


def ring(axis):
    count = lax.axis_size(axis)
    me = lax.axis_index(axis)
    return lax.rem(me + count - 1, count), lax.rem(me + 1, count)


DIRECTIONS = [
    (a, b, c)
    for a in (-1, 1, 0)
    for b in (0, -1, 1)
    for c in (0, -1, 1)
    if (a, b, c) != (0, 0, 0)
]


def slot_of(step):
    return {0: 0, -1: 1, 1: 2}[step]


def partners():
    around = {axis: (lax.axis_index(axis),) + ring(axis) for axis in ("gx", "gy", "gz")}
    return {
        d: {axis: around[axis][slot_of(step)] for axis, step in zip(("gx", "gy", "gz"), d)}
        for d in DIRECTIONS
    }


def greet(around):
    barrier = pltpu.get_barrier_semaphore()
    for target in around.values():
        pl.semaphore_signal(
            barrier, inc=1, device_id=target, device_id_type=pl.DeviceIdType.MESH
        )
    return barrier


def sender(send_sem, recv_sem):
    def send(slot, source, target, device):
        copy = pltpu.make_async_remote_copy(
            src_ref=source,
            dst_ref=target,
            send_sem=send_sem.at[slot],
            recv_sem=recv_sem.at[slot],
            device_id=device,
            device_id_type=pl.DeviceIdType.MESH,
        )
        copy.start()
        return copy

    return send


def spread_kernel(
    dims,
    spacing,
    counts_ref,
    pos_hbm,
    kind_hbm,
    feat_hbm,
    faces_hbm,
    layer_ref,
    tile_ref,
    place_ref,
    small_ref,
    pos_ref,
    kind_ref,
    feat_ref,
    faces_ref,
    out_ref,
    load_sem,
    send_sem,
    recv_sem,
):
    sx, lat, reach, o, pieces = dims
    around = partners()
    loads = [
        pltpu.make_async_copy(source, target, load_sem.at[n])
        for n, (source, target) in enumerate(
            [(pos_hbm, pos_ref), (kind_hbm, kind_ref), (feat_hbm, feat_ref), (faces_hbm, faces_ref)]
        )
    ]
    for load in loads:
        load.start()
    barrier = greet(around)
    send = sender(send_sem, recv_sem)
    for load in loads:
        load.wait()
    cx, cy, _, cz, capacity = pos_ref.shape
    sy, sz = cy * lat, cz * lat
    slot = lax.broadcasted_iota(jnp.int32, (1, capacity), 1)
    for col in range(cx):
        parts, codes = [], []
        for cell_y in range(cy):
            for cell_z in range(cz):
                xyz = [pos_ref[col, cell_y, n, cell_z : cell_z + 1] for n in range(3)]
                site = [
                    jnp.clip(jnp.floor(v * (1.0 / spacing)), 0.0, lat - 1.0) for v in xyz
                ]
                codes.append((site[0] * sy + site[1] + cell_y * lat) * sz + site[2] + cell_z * lat)
                occ = (slot < counts_ref[col, cell_z, cell_y]).astype(jnp.float32)
                kind = kind_ref[col, cell_y, cell_z : cell_z + 1].astype(jnp.float32)
                parts.append(
                    jnp.concatenate(xyz + [occ, kind, jnp.zeros((3, capacity), jnp.float32)], axis=0)
                )
        code = jnp.concatenate(codes, axis=1)
        small = jnp.concatenate(parts, axis=1)
        count = code.shape[1]
        place = (
            code == lax.broadcasted_iota(jnp.int32, (count, count), 0).astype(jnp.float32)
        ).astype(jnp.float32)
        small = lax.dot_general(
            small, place, (((1,), (1,)), ((), ())), precision=HIGH, preferred_element_type=jnp.float32
        )
        small_ref[col] = small
        tile_ref[0, 0, 0, col] = small[0:4]
        place_ref[col] = place.astype(jnp.bfloat16)
        sites = jnp.dot(place_ref[col], feat_ref[col], preferred_element_type=jnp.float32)
        sites = sites.astype(jnp.bfloat16)
        for k in range(lat):
            x = col * lat + k
            mine = sites[k * o : (k + 1) * o]
            layer_ref[reach + x, 0:o] = mine
            out_ref[x, 0:o] = mine
            faces = jnp.dot(faces_ref[...], mine, preferred_element_type=jnp.float32)
            out_ref[x, o:] = faces.astype(jnp.bfloat16)
    pl.semaphore_wait(barrier, len(around))

    from_x = {-1: pl.ds(0, reach), 1: pl.ds(sx - reach, reach), 0: pl.ds(0, sx)}
    to_x = {-1: pl.ds(reach + sx, reach), 1: pl.ds(0, reach), 0: pl.ds(reach, sx)}
    cell = {-1: pl.ds(0, 1), 1: pl.ds(cx - 1, 1), 0: pl.ds(0, cx)}
    copies = []
    for n, (a, b, c) in enumerate(DIRECTIONS):
        start, size = pieces[(b, c)]
        copies.append(
            send(
                2 * n,
                out_ref.at[from_x[a], pl.ds(start, size)],
                layer_ref.at[to_x[a], pl.ds(pieces[(-b, -c)][0], size)],
                around[(a, b, c)],
            )
        )
        copies.append(
            send(
                2 * n + 1,
                tile_ref.at[0, 0, 0, cell[a]],
                tile_ref.at[slot_of(-a), slot_of(-b), slot_of(-c), cell[a]],
                around[(a, b, c)],
            )
        )
    for copy in copies:
        copy.wait_recv()
    for copy in copies:
        copy.wait_send()


def gather_kernel(
    dims,
    place_ref,
    gsend_ref,
    gown_ref,
    force_ref,
    node_ref,
    faces_ref,
    out_ref,
    energy_ref,
    xyz_ref,
    inner_ref,
    outer_ref,
    back_ref,
    send_sem,
    recv_sem,
):
    sx, lat, reach, o, pieces = dims
    cx = sx // lat
    around = partners()
    back_ref[...] = jnp.zeros(back_ref.shape, jnp.float32)
    barrier = greet(around)
    send = sender(send_sem, recv_sem)
    pl.semaphore_wait(barrier, len(around))

    from_x = {-1: pl.ds(0, reach), 1: pl.ds(reach + sx, reach), 0: pl.ds(reach, sx)}
    cell = {-1: pl.ds(cx - 1, 1), 1: pl.ds(0, 1), 0: pl.ds(0, cx)}
    copies = []
    for n, (a, b, c) in enumerate(DIRECTIONS):
        start, size = pieces[(b, c)]
        rows = pl.ds(pieces[(-b, -c)][0], size)
        into = inner_ref.at[:, rows] if a == 0 else outer_ref.at[slot_of(-a) - 1, :, rows]
        copies.append(
            send(2 * n, gsend_ref.at[from_x[a], pl.ds(start, size)], into, around[(a, b, c)])
        )
        copies.append(
            send(
                2 * n + 1,
                force_ref.at[slot_of(a), slot_of(b), slot_of(c), cell[a]],
                back_ref.at[slot_of(-a), slot_of(-b), slot_of(-c), cell[a]],
                around[(a, b, c)],
            )
        )
    for copy in copies:
        copy.wait_recv()

    tile = node_ref[...] + force_ref[0, 0, 0]
    for a, b, c in DIRECTIONS:
        tile = tile + back_ref[slot_of(a), slot_of(b), slot_of(c)]

    def spread(received):
        return lax.dot_general(
            faces_ref[...], received, (((0,), (0,)), ((), ())), preferred_element_type=jnp.float32
        )

    _, cy, _, cz, capacity = xyz_ref.shape
    for col in range(cx):
        sites = []
        for k in range(lat):
            x = col * lat + k
            total = gown_ref[x] + spread(inner_ref[x, o:])
            for side, at in ((0, x), (1, x - (sx - reach))):
                if 0 <= at < reach:
                    total = total + outer_ref[side, at, 0:o].astype(jnp.float32)
                    total = total + spread(outer_ref[side, at, o:])
            sites.append(total)
        whole = jnp.concatenate(sites, axis=0)
        top = whole.astype(jnp.bfloat16)
        rest = (whole - top.astype(jnp.float32)).astype(jnp.bfloat16)
        place = place_ref[col].astype(jnp.float32)
        turn = place.T.astype(jnp.bfloat16)
        out_ref[col] = jnp.dot(turn, top, preferred_element_type=jnp.float32) + jnp.dot(
            turn, rest, preferred_element_type=jnp.float32
        )
        slots = jnp.dot(tile[col], place, precision=HIGH, preferred_element_type=jnp.float32)
        for n in range(cy * cz):
            lanes = slice(n * capacity, (n + 1) * capacity)
            for m in range(3):
                xyz_ref[col, n // cz, m, n % cz : n % cz + 1] = slots[m : m + 1, lanes]
            energy_ref[col, n // cz, n % cz : n % cz + 1] = slots[3:4, lanes]
    for copy in copies:
        copy.wait_send()


def tables(sx, sy, sz, reach, lat):
    px, py, depth = sx + 2 * reach, sy + 2 * reach, sz + 2 * reach
    wide, nbx, nby = BLOCK + 2 * reach, sx // BLOCK, sy // BLOCK
    o = sy * sz
    extent = {0: (sy, sz), -1: (reach, reach), 1: (reach, reach)}
    pieces, total = {}, 0
    for b in (0, -1, 1):
        for c in (0, -1, 1):
            size = extent[b][0] * extent[c][1]
            pieces[(b, c)] = (total, -(-size // 16) * 16)
            total += pieces[(b, c)][1]

    def spot(n, size):
        if n < reach:
            return -1, n
        if n >= reach + size:
            return 1, n - reach - size
        return 0, n - reach

    pick = np.zeros((nby, wide, depth, total), np.float32)
    pick_pos = np.zeros((9 * o, nby, wide, depth), np.float32)
    for by in range(nby):
        for y in range(wide):
            for z in range(depth):
                b, at_y = spot(by * BLOCK + y, sy)
                c, at_z = spot(z, sz)
                pick[by, y, z, pieces[(b, c)][0] + at_y * extent[c][1] + at_z] = 1
                tile_y = sy - reach + at_y if b < 0 else at_y
                tile_z = sz - reach + at_z if c < 0 else at_z
                line = (slot_of(b) * 3 + slot_of(c)) * o + tile_y * sz + tile_z
                pick_pos[line, by, y, z] = 1
    faces = np.zeros((total - o, o), np.float32)
    for (b, c), (start, _) in pieces.items():
        if (b, c) == (0, 0):
            continue
        for y in range(extent[b][0]):
            for z in range(extent[c][1]):
                from_y = sy - reach + y if b > 0 else y
                from_z = sz - reach + z if c > 0 else z
                faces[start - o + y * extent[c][1] + z, from_y * sz + from_z] = 1
    steps = [np.floor((np.arange(n) - reach) / lat).astype(np.float32) * SIDE for n in (px, py, depth)]
    shifts = np.zeros((px, 4, py, depth), np.float32)
    shifts[:, 0] = steps[0][:, None, None]
    shifts[:, 1] = steps[1][None, :, None]
    shifts[:, 2] = steps[2][None, None, :]
    shift = np.stack([shifts[:, :, by * BLOCK : by * BLOCK + wide] for by in range(nby)], axis=2)
    count = sx * sy * sz
    index = np.arange(count).reshape(nbx, BLOCK, nby, BLOCK, sz).transpose(2, 0, 1, 3, 4).reshape(-1)
    turn = np.zeros((count, count), np.float32)
    turn[np.arange(count), index] = 1
    inner = shifts[reach : reach + sx, :, reach : reach + sy, reach : reach + sz]
    origin = np.zeros((count, 8), np.float32)
    origin[:, :4] = inner.transpose(0, 2, 3, 1).reshape(count, 4)[index]
    return (
        pieces,
        total,
        pick.reshape(-1, total),
        pick_pos.reshape(9 * o, -1),
        faces,
        shift.reshape(px * 4, -1),
        turn,
        origin,
    )


def body(
    local_pos,
    counts,
    species,
    features,
    radial_weights,
    coupling,
    mixing,
    hidden_weights,
    output_weights,
):
    cx, cy, cz = counts.shape
    capacity, channels = features.shape[3:]
    nb = radial_weights.shape[1]
    lat, spacing, reach = lattice_of(capacity)
    sx, sy, sz = cx * lat, cy * lat, cz * lat
    nbx, nby = sx // BLOCK, sy // BLOCK
    wide, depth = BLOCK + 2 * reach, sz + 2 * reach
    near, own = wide * wide * depth, BLOCK * BLOCK * sz
    px = sx + 2 * reach
    rows = wide * depth
    blocks = nbx * nby
    o = sy * sz
    pieces, total, pick, pick_pos, faces, shift, turn, origin = tables(sx, sy, sz, reach, lat)
    column = cy * cz * capacity
    total_own = sx * sy * sz
    f32, half = jnp.float32, jnp.bfloat16

    vmem = pl.BlockSpec(memory_space=pltpu.VMEM)
    hbm = pl.BlockSpec(memory_space=pltpu.HBM)
    dims = (sx, lat, reach, o, pieces)
    limit = 61 * 1024 * 1024
    ways = 2 * len(DIRECTIONS)
    faces = jnp.asarray(faces, half)
    local_turned = local_pos.transpose(0, 1, 3, 2, 4)
    feat_flat = features.reshape(cx, column, channels)
    tile_shape = (3, 3, 3, cx, 4, lat * o)
    layers, tiles, place, small_sites = pl.pallas_call(
        functools.partial(spread_kernel, dims, spacing),
        out_shape=(
            jax.ShapeDtypeStruct((px, total, channels), half),
            jax.ShapeDtypeStruct(tile_shape, f32),
            jax.ShapeDtypeStruct((cx, column, column), half),
            jax.ShapeDtypeStruct((cx, 8, column), f32),
        ),
        in_specs=[pl.BlockSpec(memory_space=pltpu.SMEM)] + [hbm] * 4,
        out_specs=(vmem,) * 4,
        scratch_shapes=[
            pltpu.VMEM(local_turned.shape, f32),
            pltpu.VMEM(species.shape, jnp.int32),
            pltpu.VMEM(feat_flat.shape, half),
            pltpu.VMEM(faces.shape, half),
            pltpu.VMEM((sx, total, channels), half),
            pltpu.SemaphoreType.DMA((4,)),
            pltpu.SemaphoreType.DMA((ways,)),
            pltpu.SemaphoreType.DMA((ways,)),
        ],
        compiler_params=pltpu.CompilerParams(
            collective_id=0, has_side_effects=True, vmem_limit_bytes=limit
        ),
        name="halo_out",
    )(counts.transpose(0, 2, 1), local_turned, species, feat_flat, faces)

    fixed = [
        jnp.asarray(pick, half),
        jnp.asarray(pick.T, half),
        jnp.asarray(pick_pos, half),
        jnp.asarray(shift),
        jnp.asarray(turn, half),
        jnp.asarray(origin),
        radial_weights,
        coupling.transpose(1, 0, 2),
        mixing,
        hidden_weights.T,
        output_weights[None, :],
    ]
    gsend, gown, force, node = pl.pallas_call(
        functools.partial(compute_kernel, (sx, sy, sz, reach, nb, lat)),
        out_shape=(
            jax.ShapeDtypeStruct((px, total, channels), half),
            jax.ShapeDtypeStruct((sx, o, channels), f32),
            jax.ShapeDtypeStruct(tile_shape, f32),
            jax.ShapeDtypeStruct((cx, 4, lat * o), f32),
        ),
        in_specs=[vmem] * 3 + [hbm] * len(fixed),
        out_specs=(vmem,) * 4,
        scratch_shapes=[pltpu.VMEM(item.shape, item.dtype) for item in fixed]
        + [
            pltpu.VMEM((blocks, own, 8), f32),
            pltpu.VMEM((nby, px, 4, rows), f32),
            pltpu.VMEM((total_own, 128), f32),
            pltpu.VMEM((blocks, 4, near), f32),
            pltpu.VMEM((4, near), f32),
            pltpu.VMEM((nby, px, rows, channels), half),
            pltpu.VMEM((blocks // 2, nb * 4 * own, near), half),
            pltpu.VMEM((blocks // 2, nb * 4 * own, near), half),
            pltpu.VMEM((blocks, 8, own, near), f32),
            pltpu.VMEM((4, total_own, channels), f32),
            pltpu.VMEM((total_own, 128), f32),
            pltpu.VMEM((nby, px, rows, channels), f32),
            pltpu.VMEM((nb * 4 * own, near), f32),
            pltpu.VMEM((nb * 4 * own, near), f32),
            pltpu.SemaphoreType.DMA((len(fixed),)),
        ],
        compiler_params=pltpu.CompilerParams(vmem_limit_bytes=limit),
        name="pair_layer",
    )(layers, tiles, small_sites, *fixed)

    grad, energy, forces = pl.pallas_call(
        functools.partial(gather_kernel, dims),
        out_shape=(
            jax.ShapeDtypeStruct((cx, column, channels), f32),
            jax.ShapeDtypeStruct((cx, cy, cz, capacity), f32),
            jax.ShapeDtypeStruct((cx, cy, 3, cz, capacity), f32),
        ),
        in_specs=[vmem] * 6,
        out_specs=(vmem, vmem, vmem),
        scratch_shapes=[
            pltpu.VMEM((sx, total, channels), half),
            pltpu.VMEM((2, reach, total, channels), half),
            pltpu.VMEM(tile_shape, f32),
            pltpu.SemaphoreType.DMA((ways,)),
            pltpu.SemaphoreType.DMA((ways,)),
        ],
        compiler_params=pltpu.CompilerParams(
            collective_id=1, has_side_effects=True, vmem_limit_bytes=limit
        ),
        name="halo_back",
    )(place, gsend, gown, force, node, faces)
    return (
        energy,
        forces.transpose(0, 1, 3, 2, 4),
        grad.reshape(cx, cy, cz, capacity, channels),
    )


def solution(mesh):
    placed = (
        P("gx", "gy", "gz", None, None),
        P("gx", "gy", "gz"),
        P("gx", "gy", "gz", None),
        P("gx", "gy", "gz", None, None),
        P(),
        P(),
        P(),
        P(),
        P(),
    )
    return jax.shard_map(
        body,
        mesh=mesh,
        in_specs=placed,
        out_specs=(
            P("gx", "gy", "gz", None),
            P("gx", "gy", "gz", None, None),
            P("gx", "gy", "gz", None, None),
        ),
        check_vma=False,
    )
```
